32 devices in a mesh: dp: 8 (over z, y), tensor: 4 (over x, core).
Axes of the slice: x: 2, y: 2, z: 4, core: 2. Of those that a mesh axis runs over, the one named last changes fastest.
Arguments:
- tokens: bfloat16 [4096, 16384], P('dp', 'tensor'), may hold values from -6 to 6
- queries: bfloat16 [4096, 4096], P('dp', 'tensor'), as said below
- out_grad: bfloat16 [4096, 4096], P('dp', 'tensor'), may hold values from -6 to 6
- key_weight: bfloat16 [16384, 256], P('tensor'), may hold values from -0.0625 to 0.0625
- value_weight: bfloat16 [16384, 256], P('tensor'), may hold values from -0.0625 to 0.0625
- key_scale: float32 [32, 256], replicated, may hold values from 0.1 to 1.9
- value_scale: float32 [32, 256], replicated, may hold values from 0.1 to 1.9
- segment_ids: int32 [8, 512], P('dp'), may hold values from 0 to 3, never falling along the last dimension, each value on 1 to 256 neighbouring positions
- tenant_ids: int32 [8, 4], P('dp'), may hold values from 0 to 31
Outputs:
- input_grad: bfloat16 [4096, 16384], P('dp', 'tensor')
- key_scale_grad: float32 [32, 256], P(None, 'tensor')
- value_scale_grad: float32 [32, 256], P(None, 'tensor')
The draws below stay inside these ranges and needn't reach their ends.
Inputs may be any that keep to these rules, and one draw needn't show every extreme that they name: `segment_ids`: in each token group the sequence number never falls, all 4 sequences are present, and the longest holds exactly 256 tokens. `queries`: entries lie between -160 and 160.
All inputs are finite; a program needn't handle non-finite values.
Results may differ from the reference program's by a relative error of at most 0.034.
The reference program's roundings to bfloat16 on the way count: a program that leaves them out, or rounds other values in their place, can miss the bound.
Values may be sent and summed in bfloat16 or wider, within the bound.
A program may use at most 128 MiB of HBM per device.

```python
import math
import jax
import jax.numpy as jnp
import numpy as np
from jax import lax

D = 16384
HD = 128
GROUP = 16
HQ = 32
KV = 2
TOK = 512
SEQS = 4
NT = 32
GROUPS = 8
TOKENS = 4096


def draw_queries(key, part):
    key = jax.random.fold_in(key, 7)
    normal_key = jax.random.fold_in(key, 0)
    values_drawn = jax.random.normal(normal_key, (TOKENS, HQ * HD), jnp.float32)
    values_drawn = jnp.clip(values_drawn, -6.0, 6.0)
    return values_drawn.astype(jnp.bfloat16)


def plant(array, key, low, high):
    longest = array.shape.index(max(array.shape))
    spots = []
    for shift in (0, 1):
        where = [jax.random.randint(jax.random.fold_in(key, axis), (), 0, length) for axis, length in enumerate(array.shape)]
        where[longest] = (where[longest] + shift) % array.shape[longest]
        spots.append(tuple(where))
    return array.at[spots[0]].set(low).at[spots[1]].set(high)


def with_spikes(result, own_key, source, target, blocks, factor):
    def block_of(dim):
        return (jnp.arange(result.shape[dim]) // (result.shape[dim] // blocks)).reshape((-1,) + (1,) * (result.ndim - 1 - dim))

    one_side = jax.random.permutation(own_key, blocks)[block_of(target)]
    other_side = (block_of(target) + blocks // 2) % blocks
    return jnp.where((block_of(source) == one_side) | (block_of(source) == other_side), factor * result, result)


def shard_levels(own_key, dims, pieces, least, high):
    level, own = 1.0, jax.random.fold_in(own_key, 6)
    for dim, parts in pieces:
        heights = jnp.exp(jax.random.uniform(jax.random.fold_in(own, dim), (parts,), jnp.float32, least / len(pieces), high / len(pieces)))
        level = level * jnp.repeat(heights, dims[dim] // parts).reshape([-1 if axis == dim else 1 for axis in range(len(dims))])
    return level


def split_up(amount, total, limit, skew):
    weights = [(1 << 20) // math.isqrt(rank ** skew) + 1 for rank in range(2, amount + 1)]
    rest, given = total - limit - (amount - 1), [1] * (amount - 1)
    while rest > 0:
        movable = [i for i in range(amount - 1) if given[i] < limit]
        pool, left = sum([weights[i] for i in movable]), rest
        for i in movable:
            extra = min(limit - given[i], max(1, left * weights[i] // pool), rest)
            given[i] = given[i] + extra
            rest = rest - extra
    return np.array([limit] + given)


def uneven(rng, number_of, total, bound, slope):
    if number_of == 2:
        one = jax.random.randint(rng, (), max(1, total - bound), min(bound, total - 1) + 1)
        return jnp.stack([one, total - one])
    sizes = jnp.asarray(split_up(number_of, total, bound, slope), jnp.int32)
    twos = (number_of - 1) // 2
    donor, receiver = sizes[1:1 + 2 * twos:2], sizes[2:2 + 2 * twos:2]
    slack = jnp.minimum(donor - 1, bound - receiver)
    passed = jax.random.randint(jax.random.fold_in(rng, 1), (twos,), 0, 1 << 20) % (slack + 1)
    sizes = sizes.at[1:1 + 2 * twos:2].set(donor - passed).at[2:2 + 2 * twos:2].set(receiver + passed)
    return sizes[jax.random.permutation(jax.random.fold_in(rng, 2), number_of)]


def scatter_about(own_key, dims, deviation, bound, cuts=(), kind=jnp.bfloat16):
    drawn = deviation * jax.random.normal(own_key, dims, jnp.float32)
    if cuts:
        drawn = drawn * shard_levels(own_key, dims, cuts, -0.22, 0.18)
    return jnp.clip(drawn, -bound, bound).astype(kind)


def noise_with(own_key, extent, spread, most, pieces, heavy, kind=jnp.bfloat16):
    drawn = spread * jax.random.normal(own_key, extent, jnp.float32)
    if pieces:
        drawn = drawn * shard_levels(own_key, extent, pieces, -0.22, 0.18)
    return jnp.clip(with_spikes(drawn, jax.random.fold_in(own_key, 3), *heavy), -most, most).astype(kind)


def setup_inputs(seed: int = 0) -> dict:
    seeds = jax.random.split(jax.random.key(seed), 10)
    tokens = scatter_about(seeds[0], (TOKENS, D), 1.0, 6.0, ((0, 8), (1, 4)))
    queries = draw_queries(jax.random.fold_in(seeds[9], 71), 0)
    out_grad = scatter_about(seeds[2], (TOKENS, HQ * HD), 1.0, 6.0, ((0, 8), (1, 4)))
    key_weight = noise_with(seeds[3], (D, KV * HD), D ** -0.5, 0.0625, ((0, 4),), (0, 1, 4, 2.0))
    value_weight = noise_with(seeds[4], (D, KV * HD), D ** -0.5, 0.0625, ((0, 4),), (0, 1, 4, 2.0))
    key_scale = jnp.clip(1.0 + 0.18 * jax.random.normal(seeds[5], (NT, KV * HD), jnp.float32), 0.1, 1.9)
    value_scale = jnp.clip(1.0 + 0.18 * jax.random.normal(seeds[6], (NT, KV * HD), jnp.float32), 0.1, 1.9)
    segment_ids = jax.vmap(lambda own: jnp.searchsorted(jnp.cumsum(uneven(own, SEQS, TOK, TOK // 2, 0)), jnp.arange(TOK), side="right"))(jax.random.split(seeds[7], GROUPS)).reshape((GROUPS, TOK)).astype(jnp.int32)
    tenant_ids = plant(jax.random.randint(seeds[8], (GROUPS, SEQS), 0, NT), jax.random.fold_in(seeds[8], 1), 0, NT - 1).astype(jnp.int32)
    return dict(tokens=tokens, queries=queries, out_grad=out_grad, key_weight=key_weight, value_weight=value_weight, key_scale=key_scale, value_scale=value_scale, segment_ids=segment_ids, tenant_ids=tenant_ids)


def tenant_rows(segments, tenants):
    seq_match = segments[:, None] == jnp.arange(SEQS, dtype=jnp.int32)[None, :]
    tenant_tok = jnp.sum(jnp.where(seq_match, tenants[None, :], 0), axis=1).astype(jnp.int32)
    return (tenant_tok[:, None] == jnp.arange(NT, dtype=jnp.int32)[None, :]).astype(jnp.float32)


def allowed_mask(segments):
    position = jnp.arange(segments.shape[0], dtype=jnp.int32)
    return (segments[:, None] == segments[None, :]) & (position[None, :] <= position[:, None])


def head_grads(query_head, out_head, key_tile, value_tile, allowed):
    score_scale = HD ** -0.5
    scores = lax.dot_general(query_head, key_tile, (((1,), (1,)), ((), ())), preferred_element_type=jnp.float32) * score_scale
    scores = jnp.where(allowed, scores, -1e30)
    row_peak = jnp.max(scores, axis=1, keepdims=True)
    exp_scores = jnp.exp(scores - row_peak)
    probs = exp_scores / jnp.sum(exp_scores, axis=1, keepdims=True)
    probs_low = probs.astype(jnp.bfloat16)
    attended = jnp.dot(probs_low, value_tile, preferred_element_type=jnp.float32)
    row_delta = jnp.sum(out_head.astype(jnp.float32) * attended, axis=1, keepdims=True)
    prob_grad = lax.dot_general(out_head, value_tile, (((1,), (1,)), ((), ())), preferred_element_type=jnp.float32)
    score_grad = (probs * (prob_grad - row_delta)).astype(jnp.bfloat16)
    value_grad = lax.dot_general(probs_low, out_head, (((0,), (0,)), ((), ())), preferred_element_type=jnp.float32)
    key_grad = lax.dot_general(score_grad, query_head, (((0,), (0,)), ((), ())), preferred_element_type=jnp.float32) * score_scale
    return key_grad, value_grad


def group_grads(group_tokens, group_queries, group_outs, segments, tenants, key_weight, value_weight, key_scale, value_scale):
    tenant_hot = tenant_rows(segments, tenants)
    key_base = jnp.dot(group_tokens, key_weight, preferred_element_type=jnp.float32)
    value_base = jnp.dot(group_tokens, value_weight, preferred_element_type=jnp.float32)
    key_factor = jnp.dot(tenant_hot, key_scale, precision=lax.Precision.HIGHEST)
    value_factor = jnp.dot(tenant_hot, value_scale, precision=lax.Precision.HIGHEST)
    key_all = (key_base * key_factor).astype(jnp.bfloat16)
    value_all = (value_base * value_factor).astype(jnp.bfloat16)
    allowed = allowed_mask(segments)

    def one_kv(kv_index):
        key_tile = lax.dynamic_slice_in_dim(key_all, kv_index * HD, HD, 1)
        value_tile = lax.dynamic_slice_in_dim(value_all, kv_index * HD, HD, 1)

        def one_query(totals, query_index):
            column = ((kv_index * GROUP + query_index) * HD).astype(jnp.int32)
            query_head = lax.dynamic_slice_in_dim(group_queries, column, HD, 1)
            out_head = lax.dynamic_slice_in_dim(group_outs, column, HD, 1)
            key_part, value_part = head_grads(query_head, out_head, key_tile, value_tile, allowed)
            return (totals[0] + key_part, totals[1] + value_part), None

        zeros_tile = jnp.zeros((TOK, HD), jnp.float32)
        sums_out, unused = lax.scan(one_query, (zeros_tile, zeros_tile), jnp.arange(GROUP, dtype=jnp.int32))
        return sums_out

    key_heads, value_heads = lax.map(one_kv, jnp.arange(KV, dtype=jnp.int32))
    key_grad = jnp.transpose(key_heads, (1, 0, 2)).reshape(TOK, KV * HD)
    value_grad = jnp.transpose(value_heads, (1, 0, 2)).reshape(TOK, KV * HD)
    key_low = (key_grad * key_factor).astype(jnp.bfloat16)
    value_low = (value_grad * value_factor).astype(jnp.bfloat16)
    input_grad = lax.dot_general(key_low, key_weight, (((1,), (1,)), ((), ())), preferred_element_type=jnp.float32)
    input_grad = input_grad + lax.dot_general(value_low, value_weight, (((1,), (1,)), ((), ())), preferred_element_type=jnp.float32)
    key_tenant = lax.dot_general(tenant_hot, key_grad * key_base, (((0,), (0,)), ((), ())), precision=lax.Precision.HIGHEST)
    value_tenant = lax.dot_general(tenant_hot, value_grad * value_base, (((0,), (0,)), ((), ())), precision=lax.Precision.HIGHEST)
    return input_grad.astype(jnp.bfloat16), key_tenant, value_tenant


def reference(tokens, queries, out_grad, key_weight, value_weight, key_scale, value_scale, segment_ids, tenant_ids):
    grouped_tokens = tokens.reshape(GROUPS, TOK, D)
    grouped_queries = queries.reshape(GROUPS, TOK, HQ * HD)
    grouped_outs = out_grad.reshape(GROUPS, TOK, HQ * HD)

    def step_group(totals, inputs):
        group_tokens, group_queries, group_outs, segments, tenants = inputs
        input_grad, key_tenant, value_tenant = group_grads(group_tokens, group_queries, group_outs, segments, tenants, key_weight, value_weight, key_scale, value_scale)
        return (totals[0] + key_tenant, totals[1] + value_tenant), input_grad

    zeros_table = jnp.zeros((NT, KV * HD), jnp.float32)
    sums_out, grads_out = lax.scan(step_group, (zeros_table, zeros_table), (grouped_tokens, grouped_queries, grouped_outs, segment_ids, tenant_ids))
    return grads_out.reshape(TOKENS, D), sums_out[0], sums_out[1]
```

```python
import functools
import math

import jax
import jax.numpy as jnp
from jax import lax
from jax.experimental import pallas as pl
from jax.experimental.pallas import tpu as pltpu
from jax.sharding import PartitionSpec as P

MESH = pl.DeviceIdType.MESH
F32 = jnp.float32
BF16 = jnp.bfloat16
SEQS = 4
NT = 32
HD = 128
RB = 128
LONGEST = 256
VMEM_LIMIT = 48 * 1024 * 1024
KC = 4


def dot_nt(a, b):
    return lax.dot_general(a, b, (((1,), (1,)), ((), ())), preferred_element_type=F32)


def dot_nn(a, b):
    return jnp.dot(a, b, preferred_element_type=F32)


def inner(
    ndp, nten, tok_hbm, q_hbm, o_hbm, kw_hbm, vw_hbm, ks, vs, seg, tenants,
    low_out, sums_out,
    tok, q, o, kw, vw, part, from_core, from_chip, base, kv, factor, bias, grads, grads_in, lows, sums,
    sem_w, sem_t, sem_q, sem_o,
    s1, r1, s2, r2, s3, r3, s4, r4, s5, r5, s6, r6, s7, r7, sg, rg,
):
    chips = nten // 2
    rows_all, depth = tok.shape
    nb = rows_all // RB
    look = LONGEST // RB
    half = rows_all // 2
    kc = depth // KC
    d = lax.axis_index("dp")
    t = lax.axis_index("tensor")
    x = t // 2
    c = lax.rem(t, 2)
    other = 1 - c
    cf = c.astype(F32)
    partner = (d, 2 * x + other)
    peers = [(d, 2 * lax.rem(x + p, chips) + c) for p in range(1, chips)]
    groups = [lax.rem(d + i, ndp) for i in range(ndp)]

    def rows(b):
        return pl.ds(b * RB, RB)

    loads = {}
    for k in range(KC):
        ks_ = pl.ds(k * kc, kc)
        loads["k", k] = pltpu.make_async_copy(kw_hbm.at[ks_], kw.at[ks_], sem_w.at[k])
        loads["v", k] = pltpu.make_async_copy(vw_hbm.at[ks_], vw.at[ks_], sem_w.at[KC + k])
        loads["t", 0, k] = pltpu.make_async_copy(
            tok_hbm.at[pl.ds(0, half), ks_], tok.at[pl.ds(0, half), ks_], sem_t.at[k])
        loads["t", 1, k] = pltpu.make_async_copy(
            tok_hbm.at[pl.ds(half, half), ks_], tok.at[pl.ds(half, half), ks_], sem_t.at[KC + k])
    for b in range(nb):
        loads["q", b] = pltpu.make_async_copy(q_hbm.at[rows(b)], q.at[rows(b)], sem_q.at[b])
        loads["o", b] = pltpu.make_async_copy(o_hbm.at[rows(b)], o.at[rows(b)], sem_o.at[b])
    for k in range(KC):
        loads["k", k].start()
        loads["v", k].start()
        loads["t", 0, k].start()
    for k in range(KC):
        loads["t", 1, k].start()
    for b in range(nb):
        loads["q", b].start()
        loads["o", b].start()

    barrier = pltpu.get_barrier_semaphore()
    count = 0
    for dev in [partner] + peers:
        pl.semaphore_signal(barrier, inc=1, device_id=dev, device_id_type=MESH)
        count += 1
    for i in range(1, ndp):
        for core in range(2):
            pl.semaphore_signal(barrier, inc=1, device_id=(groups[i], 2 * x + core), device_id_type=MESH)
            count += 1

    def send(src, dst, ssem, rsem, dev):
        copy = pltpu.make_async_remote_copy(
            src_ref=src, dst_ref=dst, send_sem=ssem, recv_sem=rsem, device_id=dev, device_id_type=MESH)
        copy.start()
        return copy

    def arrived(dst, rsem):
        pltpu.make_async_remote_copy(
            src_ref=dst, dst_ref=dst, send_sem=s1.at[0], recv_sem=rsem, device_id=partner, device_id_type=MESH
        ).wait_recv()

    sent = []

    segments = seg[...]
    counts = [jnp.sum(jnp.where(segments == s, 1.0, 0.0), axis=1, keepdims=True) for s in range(SEQS)]
    bounds = [jnp.zeros((1, 1), F32)]
    for s in range(SEQS):
        bounds.append(bounds[-1] + counts[s])
    start = jnp.zeros(segments.shape, F32)
    for s in range(1, SEQS):
        start = jnp.where(segments == s, bounds[s], start)
    own_cols = pl.ds(pl.multiple_of(x * HD, HD), HD)
    own_scale = ks[:, own_cols] * (1.0 - cf) + vs[:, own_cols] * cf
    tenant = lax.broadcasted_iota(jnp.int32, (NT, HD), 0)
    scale_rows = [
        jnp.sum(jnp.where(tenant == tenants[0, s], own_scale, 0.0), axis=0, keepdims=True) for s in range(SEQS)]

    def position(b):
        return lax.broadcasted_iota(jnp.int32, (RB, HD), 0).astype(F32) + float(b * RB)

    for b in range(nb):
        pos = position(b)
        f = jnp.broadcast_to(scale_rows[SEQS - 1], (RB, HD))
        for s in range(SEQS - 2, -1, -1):
            f = jnp.where(pos < bounds[s + 1], scale_rows[s], f)
        factor[rows(b), :] = f
        grads[0, rows(b), :] = jnp.zeros((RB, HD), F32)
        grads[1, rows(b), :] = jnp.zeros((RB, HD), F32)

    pl.semaphore_wait(barrier, count)

    def project(r):
        rr = pl.ds(r * half, half)
        for k in range(KC):
            kk = pl.ds(k * kc, kc)
            if r == 0:
                loads["k", k].wait()
                loads["v", k].wait()
            loads["t", r, k].wait()
            block = tok[rr, kk]
            for kind, weight in ((0, kw), (1, vw)):
                value = dot_nn(block, weight[kk, :])
                for h in range(chips):
                    piece = value[:, h * HD:(h + 1) * HD]
                    if k:
                        piece = piece + part[kind, h, rr, :]
                    part[kind, h, rr, :] = piece

    def to_core(b):
        sent.append(send(part.at[other, :, rows(b)], from_core.at[:, rows(b)], s1.at[b], r1.at[b], partner))

    def to_chips(b):
        arrived(from_core.at[:, rows(b)], r1.at[b])
        for p in range(1, chips):
            j = lax.rem(x + p, chips)
            part[c, j, rows(b), :] = part[c, j, rows(b), :] + from_core[j, rows(b), :]
            i = (p - 1) * nb + b
            sent.append(send(part.at[c, j, rows(b)], from_chip.at[p - 1, rows(b)], s2.at[i], r2.at[i], peers[p - 1]))

    def finish(b):
        total = part[c, x, rows(b), :] + from_core[x, rows(b), :]
        for p in range(1, chips):
            arrived(from_chip.at[p - 1, rows(b)], r2.at[(p - 1) * nb + b])
            total = total + from_chip[p - 1, rows(b), :]
        base[rows(b), :] = total
        kv[c, rows(b), :] = (total * factor[rows(b), :]).astype(BF16)
        sent.append(send(kv.at[c, rows(b)], kv.at[c, rows(b)], s3.at[b], r3.at[b], partner))

    heads = q.shape[1] // HD
    score_scale = HD ** -0.5
    to_exp2 = score_scale * math.log2(math.e)

    def ready(b):
        arrived(kv.at[other, rows(b)], r3.at[b])
        loads["q", b].wait()
        loads["o", b].wait()
        first = max(0, b - look)
        query_pos = lax.broadcasted_iota(jnp.int32, (RB, RB), 1).astype(F32) + float(b * RB)
        begin = start[:, b * RB:(b + 1) * RB]
        for j in range(first, b + 1):
            key_pos = position(j)
            seen = (key_pos >= begin) & (key_pos <= query_pos)
            bias[rows(j - first), :] = jnp.where(seen, 0.0, -1e30)

    def attend(b, lo, hi):
        first = max(0, b - look)
        width = (b + 1 - first) * RB
        keys_at = pl.ds(first * RB, width)

        def pair(i, _):
            c0 = pl.multiple_of(i * 2 * HD, 2 * HD)
            c1 = pl.multiple_of(i * 2 * HD + HD, HD)
            qh = jnp.concatenate([q[rows(b), pl.ds(c0, HD)], q[rows(b), pl.ds(c1, HD)]], axis=0)
            oh = jnp.concatenate([o[rows(b), pl.ds(c0, HD)], o[rows(b), pl.ds(c1, HD)]], axis=0)
            hidden = bias[pl.ds(0, width), :]
            scores = dot_nt(kv[0, keys_at, :], qh) + jnp.concatenate([hidden, hidden], axis=1)
            grad = dot_nt(kv[1, keys_at, :], oh)
            peak = jnp.max(scores, axis=0, keepdims=True)
            e = jnp.exp2((scores - peak) * to_exp2)
            probs = e * (1.0 / jnp.sum(e, axis=0, keepdims=True))
            low = probs.astype(BF16)
            delta = jnp.sum(low.astype(F32) * grad, axis=0, keepdims=True)
            score_grad = (probs * (grad - delta)).astype(BF16)
            grads[1, keys_at, :] = grads[1, keys_at, :] + dot_nn(low, oh)
            grads[0, keys_at, :] = grads[0, keys_at, :] + dot_nn(score_grad, qh)
            return 0

        lax.fori_loop(lo, hi, pair, 0)

    def grads_to_core(b):
        sent.append(send(grads.at[other, rows(b)], grads_in.at[rows(b)], s4.at[b], r4.at[b], partner))

    tables = [jnp.zeros((1, HD), F32) for s in range(SEQS)]

    def lows_out(b):
        arrived(grads_in.at[rows(b)], r4.at[b])
        total = (grads[c, rows(b), :] + grads_in[rows(b), :]) * (cf + (1.0 - cf) * score_scale)
        lows[c, x, rows(b), :] = (total * factor[rows(b), :]).astype(BF16)
        for p in range(1, chips):
            i = (p - 1) * nb + b
            sent.append(send(lows.at[c, x, rows(b)], lows.at[c, x, rows(b)], s6.at[i], r6.at[i], peers[p - 1]))
        sent.append(send(lows.at[c, x, rows(b)], lows.at[c, x, rows(b)], s5.at[b], r5.at[b], partner))
        product = total * base[rows(b), :]
        pos = position(b)
        for s in range(SEQS):
            inside = (pos >= bounds[s]) & (pos < bounds[s + 1])
            tables[s] = tables[s] + jnp.sum(jnp.where(inside, product, 0.0), axis=0, keepdims=True)

    def forward(b):
        for p in range(1, chips):
            j = lax.rem(x + chips - p, chips)
            i = (p - 1) * nb + b
            arrived(lows.at[c, j, rows(b)], r6.at[i])
            sent.append(send(lows.at[c, j, rows(b)], lows.at[c, j, rows(b)], s7.at[i], r7.at[i], partner))

    for r in range(2):
        project(r)
        for b in range(r * nb // 2, (r + 1) * nb // 2):
            to_core(b)
        if r == 0:
            for b in range(nb // 2):
                to_chips(b)
    for b in range(nb // 2, nb):
        to_chips(b)
    finish(0)
    finish(1)
    pairs = heads // 2
    for b in range(nb):
        ready(b)
        last = b == nb - 1
        attend(b, 0, pairs // 2 if last else pairs)
        if b + 2 < nb:
            finish(b + 2)
        if last:
            for j in range(nb - 1 - look):
                lows_out(j)
            attend(b, pairs // 2, pairs)
        elif b >= look:
            grads_to_core(b - look)
    for j in range(nb - 1 - look, nb):
        grads_to_core(j)
    for j in range(nb - 1 - look, nb):
        lows_out(j)

    for s in range(SEQS):
        sums[0, c, pl.ds(s, 1), :] = tables[s]
        sums[0, c, pl.ds(SEQS + s, 1), :] = jnp.full((1, HD), 1.0, F32) * tenants[0, s].astype(F32)
    for i in range(ndp):
        if i == 0:
            sent.append(send(sums.at[0, c], sums.at[0, c], sg.at[other], rg.at[c], partner))
        else:
            for core in range(2):
                sent.append(send(
                    sums.at[0, c], sums.at[i, c], sg.at[2 * i + core], rg.at[2 * i + c], (groups[i], 2 * x + core)))
    for b in range(nb):
        forward(b)
    for b in range(nb):
        arrived(lows.at[other, x, rows(b)], r5.at[b])
        for p in range(1, chips):
            j = lax.rem(x + chips - p, chips)
            arrived(lows.at[other, j, rows(b)], r7.at[(p - 1) * nb + b])
    for kind in range(2):
        for h in range(chips):
            low_out[:, pl.ds((kind * chips + h) * HD, HD)] = lows[kind, h]
    for i in range(ndp):
        if i == 0:
            arrived(sums.at[0, other], rg.at[other])
        else:
            for core in range(2):
                arrived(sums.at[i, core], rg.at[2 * i + core])
    for i in range(ndp):
        for core in range(2):
            value = sums[i, core]
            turned = jnp.concatenate([value[:, HD // 2:], value[:, :HD // 2]], axis=1)
            sums_out[i, core] = value * (1.0 - cf) + turned * cf
    for copy in sent:
        copy.wait_send()


def closing(ndp, low, kw, vw, sums, grad_out, key_out, value_out):
    wide = kw.shape[1]
    grad = dot_nt(low[:, :wide], kw[...]) + dot_nt(low[:, wide:], vw[...])
    grad_out[...] = grad.astype(BF16)

    @pl.when(pl.program_id(0) == 0)
    def _():
        tenant = lax.broadcasted_iota(jnp.int32, (NT, HD), 0).astype(F32)
        for kind, out in ((0, key_out), (1, value_out)):
            total = jnp.zeros((NT, HD), F32)
            for i in range(ndp):
                block = sums[i, kind]
                for s in range(SEQS):
                    total = total + jnp.where(tenant == block[SEQS + s:SEQS + s + 1, :], block[s:s + 1, :], 0.0)
            out[...] = total[:, :HD // 2]


def on_device(ndp, nten, tokens, queries, out_grad, key_weight, value_weight, key_scale, value_scale, segment_ids, tenant_ids):
    chips = nten // 2
    rows_all, depth = tokens.shape
    nb = rows_all // RB
    wide = key_weight.shape[1]
    anywhere = pl.BlockSpec(memory_space=pl.ANY)
    vmem = pl.BlockSpec(memory_space=pltpu.VMEM)
    smem = pl.BlockSpec(memory_space=pltpu.SMEM)
    sem = pltpu.SemaphoreType.DMA
    many = max(1, (chips - 1) * nb)
    low, sums = pl.pallas_call(
        functools.partial(inner, ndp, nten),
        out_shape=(
            jax.ShapeDtypeStruct((rows_all, 2 * wide), BF16),
            jax.ShapeDtypeStruct((ndp, 2, 2 * SEQS, HD), F32),
        ),
        in_specs=[anywhere] * 5 + [vmem] * 3 + [smem],
        out_specs=(vmem, vmem),
        scratch_shapes=[
            pltpu.VMEM(tokens.shape, BF16),
            pltpu.VMEM(queries.shape, BF16),
            pltpu.VMEM(out_grad.shape, BF16),
            pltpu.VMEM(key_weight.shape, BF16),
            pltpu.VMEM(value_weight.shape, BF16),
            pltpu.VMEM((2, chips, rows_all, HD), F32),
            pltpu.VMEM((chips, rows_all, HD), F32),
            pltpu.VMEM((max(1, chips - 1), rows_all, HD), F32),
            pltpu.VMEM((rows_all, HD), F32),
            pltpu.VMEM((2, rows_all, HD), BF16),
            pltpu.VMEM((rows_all, HD), F32),
            pltpu.VMEM((LONGEST + RB, RB), F32),
            pltpu.VMEM((2, rows_all, HD), F32),
            pltpu.VMEM((rows_all, HD), F32),
            pltpu.VMEM((2, chips, rows_all, HD), BF16),
            pltpu.VMEM((ndp, 2, 2 * SEQS, HD), F32),
            sem((2 * KC,)), sem((2 * KC,)), sem((nb,)), sem((nb,)),
            sem((nb,)), sem((nb,)), sem((many,)), sem((many,)), sem((nb,)), sem((nb,)), sem((nb,)), sem((nb,)),
            sem((nb,)), sem((nb,)), sem((many,)), sem((many,)), sem((many,)), sem((many,)),
            sem((2 * ndp,)), sem((2 * ndp,)),
        ],
        compiler_params=pltpu.CompilerParams(
            collective_id=0, has_side_effects=True, vmem_limit_bytes=VMEM_LIMIT),
    )(tokens, queries, out_grad, key_weight, value_weight, key_scale, value_scale, segment_ids, tenant_ids)

    block = min(512, depth)
    return pl.pallas_call(
        functools.partial(closing, ndp),
        grid=(depth // block,),
        out_shape=(
            jax.ShapeDtypeStruct((rows_all, depth), BF16),
            jax.ShapeDtypeStruct((NT, HD // 2), F32),
            jax.ShapeDtypeStruct((NT, HD // 2), F32),
        ),
        in_specs=[
            pl.BlockSpec((rows_all, 2 * wide), lambda i: (0, 0)),
            pl.BlockSpec((block, wide), lambda i: (i, 0)),
            pl.BlockSpec((block, wide), lambda i: (i, 0)),
            pl.BlockSpec((ndp, 2, 2 * SEQS, HD), lambda i: (0, 0, 0, 0)),
        ],
        out_specs=(
            pl.BlockSpec((rows_all, block), lambda i: (0, i)),
            pl.BlockSpec((NT, HD // 2), lambda i: (0, 0)),
            pl.BlockSpec((NT, HD // 2), lambda i: (0, 0)),
        ),
        compiler_params=pltpu.CompilerParams(vmem_limit_bytes=VMEM_LIMIT),
    )(low, key_weight, value_weight, sums)


def solution(mesh):
    return jax.shard_map(
        functools.partial(on_device, mesh.shape["dp"], mesh.shape["tensor"]),
        mesh=mesh,
        in_specs=(
            P("dp", "tensor"),
            P("dp", "tensor"),
            P("dp", "tensor"),
            P("tensor", None),
            P("tensor", None),
            P(),
            P(),
            P("dp", None),
            P("dp", None),
        ),
        out_specs=(P("dp", "tensor"), P(None, "tensor"), P(None, "tensor")),
        check_vma=False,
    )
```

```python
import functools
import math

import jax
import jax.numpy as jnp
from jax import lax
from jax.experimental import pallas as pl
from jax.experimental.pallas import tpu as pltpu
from jax.sharding import PartitionSpec as P

MESH = pl.DeviceIdType.MESH
F32 = jnp.float32
BF16 = jnp.bfloat16
SEQS = 4
NT = 32
HD = 128
RB = 128
LONGEST = 256
VMEM_LIMIT = 64 * 1024 * 1024
TOGETHER = 4
KC = 4


def dot_nt(a, b):
    return lax.dot_general(a, b, (((1,), (1,)), ((), ())), preferred_element_type=F32)


def dot_nn(a, b):
    return jnp.dot(a, b, preferred_element_type=F32)


def inner(
    ndp, nten, tok_hbm, q_hbm, o_hbm, kw_hbm, vw_hbm, ks_hbm, vs_hbm, seg_hbm, tenants_hbm,
    low_out, sums_out,
    tok, q, o, kw, vw, part, from_core, from_chip, base, kv, factor, bias, grads, grads_in, lows, sums,
    ks, vs, seg, tenants,
    sem_w, sem_t, sem_q, sem_o, sem_p,
    s1, r1, s2, r2, s3, r3, s4, r4, s5, r5, s6, r6, s7, r7, sg, rg,
):
    chips = nten // 2
    rows_all, depth = tok.shape
    nb = rows_all // RB
    look = LONGEST // RB
    half = rows_all // 2
    kc = depth // KC
    d = lax.axis_index("dp")
    t = lax.axis_index("tensor")
    x = t // 2
    c = lax.rem(t, 2)
    other = 1 - c
    cf = c.astype(F32)
    partner = (d, 2 * x + other)
    peers = [(d, 2 * lax.rem(x + p, chips) + c) for p in range(1, chips)]
    groups = [lax.rem(d + i, ndp) for i in range(ndp)]

    def rows(b):
        return pl.ds(b * RB, RB)

    loads = {}
    for k in range(KC):
        ks_ = pl.ds(k * kc, kc)
        loads["k", k] = pltpu.make_async_copy(kw_hbm.at[ks_], kw.at[ks_], sem_w.at[k])
        loads["v", k] = pltpu.make_async_copy(vw_hbm.at[ks_], vw.at[ks_], sem_w.at[KC + k])
        loads["t", 0, k] = pltpu.make_async_copy(
            tok_hbm.at[pl.ds(0, half), ks_], tok.at[pl.ds(0, half), ks_], sem_t.at[k])
        loads["t", 1, k] = pltpu.make_async_copy(
            tok_hbm.at[pl.ds(half, half), ks_], tok.at[pl.ds(half, half), ks_], sem_t.at[KC + k])
    for b in range(nb):
        loads["q", b] = pltpu.make_async_copy(q_hbm.at[rows(b)], q.at[rows(b)], sem_q.at[b])
        loads["o", b] = pltpu.make_async_copy(o_hbm.at[rows(b)], o.at[rows(b)], sem_o.at[b])
    small = [
        pltpu.make_async_copy(src, dst, sem_p.at[i])
        for i, (src, dst) in enumerate(((ks_hbm, ks), (vs_hbm, vs), (seg_hbm, seg), (tenants_hbm, tenants)))]
    for copy in small:
        copy.start()
    for k in range(KC):
        loads["k", k].start()
        loads["v", k].start()
        loads["t", 0, k].start()
    for k in range(KC):
        loads["t", 1, k].start()
    for b in range(nb):
        loads["q", b].start()
        loads["o", b].start()

    barrier = pltpu.get_barrier_semaphore()
    count = 0
    for dev in [partner] + peers:
        pl.semaphore_signal(barrier, inc=1, device_id=dev, device_id_type=MESH)
        count += 1
    for i in range(1, ndp):
        for core in range(2):
            pl.semaphore_signal(barrier, inc=1, device_id=(groups[i], 2 * x + core), device_id_type=MESH)
            count += 1

    def send(src, dst, ssem, rsem, dev):
        copy = pltpu.make_async_remote_copy(
            src_ref=src, dst_ref=dst, send_sem=ssem, recv_sem=rsem, device_id=dev, device_id_type=MESH)
        copy.start()
        return copy

    def arrived(dst, rsem):
        pltpu.make_async_remote_copy(
            src_ref=dst, dst_ref=dst, send_sem=s1.at[0], recv_sem=rsem, device_id=partner, device_id_type=MESH
        ).wait_recv()

    sent = []

    for copy in small:
        copy.wait()
    segments = seg[...]
    counts = [jnp.sum(jnp.where(segments == s, 1.0, 0.0), axis=1, keepdims=True) for s in range(SEQS)]
    bounds = [jnp.zeros((1, 1), F32)]
    for s in range(SEQS):
        bounds.append(bounds[-1] + counts[s])
    start = jnp.zeros(segments.shape, F32)
    for s in range(1, SEQS):
        start = jnp.where(segments == s, bounds[s], start)
    own_cols = pl.ds(pl.multiple_of(x * HD, HD), HD)
    own_scale = ks[:, own_cols] * (1.0 - cf) + vs[:, own_cols] * cf
    tenant = lax.broadcasted_iota(jnp.int32, (NT, HD), 0)
    scale_rows = [
        jnp.sum(jnp.where(tenant == tenants[0, s], own_scale, 0.0), axis=0, keepdims=True) for s in range(SEQS)]

    def position(b):
        return lax.broadcasted_iota(jnp.int32, (RB, HD), 0).astype(F32) + float(b * RB)

    for b in range(nb):
        pos = position(b)
        f = jnp.broadcast_to(scale_rows[SEQS - 1], (RB, HD))
        for s in range(SEQS - 2, -1, -1):
            f = jnp.where(pos < bounds[s + 1], scale_rows[s], f)
        factor[rows(b), :] = f
        grads[0, rows(b), :] = jnp.zeros((RB, HD), F32)
        grads[1, rows(b), :] = jnp.zeros((RB, HD), F32)

    pl.semaphore_wait(barrier, count)

    def project(r):
        rr = pl.ds(r * half, half)
        for k in range(KC):
            kk = pl.ds(k * kc, kc)
            if r == 0:
                loads["k", k].wait()
                loads["v", k].wait()
            loads["t", r, k].wait()
            block = tok[rr, kk]
            for kind, weight in ((0, kw), (1, vw)):
                value = dot_nn(block, weight[kk, :])
                for h in range(chips):
                    piece = value[:, h * HD:(h + 1) * HD]
                    if k:
                        piece = piece + part[kind, h, rr, :]
                    part[kind, h, rr, :] = piece

    def to_core(b):
        sent.append(send(part.at[other, :, rows(b)], from_core.at[:, rows(b)], s1.at[b], r1.at[b], partner))

    def to_chips(b):
        arrived(from_core.at[:, rows(b)], r1.at[b])
        for p in range(1, chips):
            j = lax.rem(x + p, chips)
            part[c, j, rows(b), :] = part[c, j, rows(b), :] + from_core[j, rows(b), :]
            i = (p - 1) * nb + b
            sent.append(send(part.at[c, j, rows(b)], from_chip.at[p - 1, rows(b)], s2.at[i], r2.at[i], peers[p - 1]))

    def finish(b):
        total = part[c, x, rows(b), :] + from_core[x, rows(b), :]
        for p in range(1, chips):
            arrived(from_chip.at[p - 1, rows(b)], r2.at[(p - 1) * nb + b])
            total = total + from_chip[p - 1, rows(b), :]
        base[rows(b), :] = total
        kv[c, rows(b), :] = (total * factor[rows(b), :]).astype(BF16)
        sent.append(send(kv.at[c, rows(b)], kv.at[c, rows(b)], s3.at[b], r3.at[b], partner))

    heads = q.shape[1] // HD
    score_scale = HD ** -0.5
    to_exp2 = score_scale * math.log2(math.e)

    def ready(b):
        arrived(kv.at[other, rows(b)], r3.at[b])
        loads["q", b].wait()
        loads["o", b].wait()
        first = max(0, b - look)
        query_pos = lax.broadcasted_iota(jnp.int32, (RB, RB), 1).astype(F32) + float(b * RB)
        begin = start[:, b * RB:(b + 1) * RB]
        for j in range(first, b + 1):
            key_pos = position(j)
            seen = (key_pos >= begin) & (key_pos <= query_pos)
            bias[rows(j - first), :] = jnp.where(seen, 0.0, -1e30)

    def attend(b, lo, hi):
        first = max(0, b - look)
        width = (b + 1 - first) * RB
        keys_at = pl.ds(first * RB, width)

        def several(i, _):
            cols = [pl.ds(pl.multiple_of((i * TOGETHER + n) * HD, HD), HD) for n in range(TOGETHER)]
            qh = jnp.concatenate([q[rows(b), col] for col in cols], axis=0)
            oh = jnp.concatenate([o[rows(b), col] for col in cols], axis=0)
            hidden = bias[pl.ds(0, width), :]
            scores = dot_nt(kv[0, keys_at, :], qh) + jnp.concatenate([hidden] * TOGETHER, axis=1)
            grad = dot_nt(kv[1, keys_at, :], oh)
            peak = jnp.max(scores, axis=0, keepdims=True)
            e = jnp.exp2((scores - peak) * to_exp2)
            probs = e * (1.0 / jnp.sum(e, axis=0, keepdims=True))
            low = probs.astype(BF16)
            delta = jnp.sum(low.astype(F32) * grad, axis=0, keepdims=True)
            score_grad = (probs * (grad - delta)).astype(BF16)
            grads[1, keys_at, :] = grads[1, keys_at, :] + dot_nn(low, oh)
            grads[0, keys_at, :] = grads[0, keys_at, :] + dot_nn(score_grad, qh)
            return 0

        lax.fori_loop(lo, hi, several, 0)

    def grads_to_core(b):
        sent.append(send(grads.at[other, rows(b)], grads_in.at[rows(b)], s4.at[b], r4.at[b], partner))

    tables = [jnp.zeros((1, HD), F32) for s in range(SEQS)]

    def lows_out(b):
        arrived(grads_in.at[rows(b)], r4.at[b])
        total = (grads[c, rows(b), :] + grads_in[rows(b), :]) * (cf + (1.0 - cf) * score_scale)
        lows[c, x, rows(b), :] = (total * factor[rows(b), :]).astype(BF16)
        for p in range(1, chips):
            i = (p - 1) * nb + b
            sent.append(send(lows.at[c, x, rows(b)], lows.at[c, x, rows(b)], s6.at[i], r6.at[i], peers[p - 1]))
        sent.append(send(lows.at[c, x, rows(b)], lows.at[c, x, rows(b)], s5.at[b], r5.at[b], partner))
        product = total * base[rows(b), :]
        pos = position(b)
        for s in range(SEQS):
            inside = (pos >= bounds[s]) & (pos < bounds[s + 1])
            tables[s] = tables[s] + jnp.sum(jnp.where(inside, product, 0.0), axis=0, keepdims=True)

    def forward(b):
        for p in range(1, chips):
            j = lax.rem(x + chips - p, chips)
            i = (p - 1) * nb + b
            arrived(lows.at[c, j, rows(b)], r6.at[i])
            sent.append(send(lows.at[c, j, rows(b)], lows.at[c, j, rows(b)], s7.at[i], r7.at[i], partner))

    for r in range(2):
        project(r)
        for b in range(r * nb // 2, (r + 1) * nb // 2):
            to_core(b)
        if r == 0:
            for b in range(nb // 2):
                to_chips(b)
    for b in range(nb // 2, nb):
        to_chips(b)
    finish(0)
    finish(1)
    pairs = heads // TOGETHER
    for b in range(nb):
        ready(b)
        last = b == nb - 1
        attend(b, 0, pairs // 2 if last else pairs)
        if b + 2 < nb:
            finish(b + 2)
        if last:
            for j in range(nb - 1 - look):
                lows_out(j)
            attend(b, pairs // 2, pairs)
        elif b >= look:
            grads_to_core(b - look)
    for j in range(nb - 1 - look, nb):
        grads_to_core(j)
    for j in range(nb - 1 - look, nb):
        lows_out(j)

    for s in range(SEQS):
        sums[0, c, pl.ds(s, 1), :] = tables[s]
        sums[0, c, pl.ds(SEQS + s, 1), :] = jnp.full((1, HD), 1.0, F32) * tenants[0, s].astype(F32)
    for i in range(ndp):
        if i == 0:
            sent.append(send(sums.at[0, c], sums.at[0, c], sg.at[other], rg.at[c], partner))
        else:
            for core in range(2):
                sent.append(send(
                    sums.at[0, c], sums.at[i, c], sg.at[2 * i + core], rg.at[2 * i + c], (groups[i], 2 * x + core)))
    for b in range(nb):
        forward(b)
    for b in range(nb):
        arrived(lows.at[other, x, rows(b)], r5.at[b])
        for p in range(1, chips):
            j = lax.rem(x + chips - p, chips)
            arrived(lows.at[other, j, rows(b)], r7.at[(p - 1) * nb + b])
    for kind in range(2):
        for h in range(chips):
            low_out[:, pl.ds((kind * chips + h) * HD, HD)] = lows[kind, h]
    for i in range(ndp):
        if i == 0:
            arrived(sums.at[0, other], rg.at[other])
        else:
            for core in range(2):
                arrived(sums.at[i, core], rg.at[2 * i + core])
    for i in range(ndp):
        for core in range(2):
            value = sums[i, core]
            turned = jnp.concatenate([value[:, HD // 2:], value[:, :HD // 2]], axis=1)
            sums_out[i, core] = value * (1.0 - cf) + turned * cf
    for copy in sent:
        copy.wait_send()


def closing(ndp, low, kw, vw, sums, grad_out, key_out, value_out):
    wide = kw.shape[1]
    grad = dot_nt(low[:, :wide], kw[...]) + dot_nt(low[:, wide:], vw[...])
    grad_out[...] = grad.astype(BF16)

    @pl.when(pl.program_id(0) == 0)
    def _():
        tenant = lax.broadcasted_iota(jnp.int32, (NT, HD), 0).astype(F32)
        for kind, out in ((0, key_out), (1, value_out)):
            total = jnp.zeros((NT, HD), F32)
            for i in range(ndp):
                block = sums[i, kind]
                for s in range(SEQS):
                    total = total + jnp.where(tenant == block[SEQS + s:SEQS + s + 1, :], block[s:s + 1, :], 0.0)
            out[...] = total[:, :HD // 2]


def on_device(ndp, nten, tokens, queries, out_grad, key_weight, value_weight, key_scale, value_scale, segment_ids, tenant_ids):
    chips = nten // 2
    rows_all, depth = tokens.shape
    nb = rows_all // RB
    wide = key_weight.shape[1]
    hbm = pl.BlockSpec(memory_space=pltpu.HBM)
    vmem = pl.BlockSpec(memory_space=pltpu.VMEM)
    sem = pltpu.SemaphoreType.DMA
    many = max(1, (chips - 1) * nb)
    low, sums = pl.pallas_call(
        functools.partial(inner, ndp, nten),
        out_shape=(
            jax.ShapeDtypeStruct((rows_all, 2 * wide), BF16),
            jax.ShapeDtypeStruct((ndp, 2, 2 * SEQS, HD), F32),
        ),
        in_specs=[hbm] * 9,
        out_specs=(vmem, vmem),
        scratch_shapes=[
            pltpu.VMEM(tokens.shape, BF16),
            pltpu.VMEM(queries.shape, BF16),
            pltpu.VMEM(out_grad.shape, BF16),
            pltpu.VMEM(key_weight.shape, BF16),
            pltpu.VMEM(value_weight.shape, BF16),
            pltpu.VMEM((2, chips, rows_all, HD), F32),
            pltpu.VMEM((chips, rows_all, HD), F32),
            pltpu.VMEM((max(1, chips - 1), rows_all, HD), F32),
            pltpu.VMEM((rows_all, HD), F32),
            pltpu.VMEM((2, rows_all, HD), BF16),
            pltpu.VMEM((rows_all, HD), F32),
            pltpu.VMEM((LONGEST + RB, RB), F32),
            pltpu.VMEM((2, rows_all, HD), F32),
            pltpu.VMEM((rows_all, HD), F32),
            pltpu.VMEM((2, chips, rows_all, HD), BF16),
            pltpu.VMEM((ndp, 2, 2 * SEQS, HD), F32),
            pltpu.VMEM(key_scale.shape, F32),
            pltpu.VMEM(value_scale.shape, F32),
            pltpu.VMEM(segment_ids.shape, jnp.int32),
            pltpu.SMEM(tenant_ids.shape, jnp.int32),
            sem((2 * KC,)), sem((2 * KC,)), sem((nb,)), sem((nb,)), sem((4,)),
            sem((nb,)), sem((nb,)), sem((many,)), sem((many,)), sem((nb,)), sem((nb,)), sem((nb,)), sem((nb,)),
            sem((nb,)), sem((nb,)), sem((many,)), sem((many,)), sem((many,)), sem((many,)),
            sem((2 * ndp,)), sem((2 * ndp,)),
        ],
        compiler_params=pltpu.CompilerParams(
            collective_id=0, has_side_effects=True, vmem_limit_bytes=VMEM_LIMIT),
    )(tokens, queries, out_grad, key_weight, value_weight, key_scale, value_scale, segment_ids, tenant_ids)

    block = min(1024, depth)
    return pl.pallas_call(
        functools.partial(closing, ndp),
        grid=(depth // block,),
        out_shape=(
            jax.ShapeDtypeStruct((rows_all, depth), BF16),
            jax.ShapeDtypeStruct((NT, HD // 2), F32),
            jax.ShapeDtypeStruct((NT, HD // 2), F32),
        ),
        in_specs=[
            pl.BlockSpec((rows_all, 2 * wide), lambda i: (0, 0)),
            pl.BlockSpec((block, wide), lambda i: (i, 0)),
            pl.BlockSpec((block, wide), lambda i: (i, 0)),
            pl.BlockSpec((ndp, 2, 2 * SEQS, HD), lambda i: (0, 0, 0, 0)),
        ],
        out_specs=(
            pl.BlockSpec((rows_all, block), lambda i: (0, i)),
            pl.BlockSpec((NT, HD // 2), lambda i: (0, 0)),
            pl.BlockSpec((NT, HD // 2), lambda i: (0, 0)),
        ),
        compiler_params=pltpu.CompilerParams(vmem_limit_bytes=VMEM_LIMIT),
    )(low, key_weight, value_weight, sums)


def solution(mesh):
    return jax.shard_map(
        functools.partial(on_device, mesh.shape["dp"], mesh.shape["tensor"]),
        mesh=mesh,
        in_specs=(
            P("dp", "tensor"),
            P("dp", "tensor"),
            P("dp", "tensor"),
            P("tensor", None),
            P("tensor", None),
            P(),
            P(),
            P("dp", None),
            P("dp", None),
        ),
        out_specs=(P("dp", "tensor"), P(None, "tensor"), P(None, "tensor")),
        check_vma=False,
    )
```

```python
import functools
import math

import jax
import jax.numpy as jnp
from jax import lax
from jax.experimental import pallas as pl
from jax.experimental.pallas import tpu as pltpu
from jax.sharding import PartitionSpec as P

MESH = pl.DeviceIdType.MESH
F32 = jnp.float32
BF16 = jnp.bfloat16
SEQS = 4
NT = 32
HD = 128
RB = 128
LONGEST = 256
VMEM_LIMIT = 64 * 1024 * 1024
TOGETHER = 4
KC = 4


def dot_nt(a, b):
    return lax.dot_general(a, b, (((1,), (1,)), ((), ())), preferred_element_type=F32)


def dot_nn(a, b):
    return jnp.dot(a, b, preferred_element_type=F32)


def inner(
    ndp, nten, tok_hbm, q_hbm, o_hbm, kw_hbm, vw_hbm, ks_hbm, vs_hbm, seg_hbm, tenants_hbm,
    low_out, sums_out,
    tok, q, o, kw, vw, part, from_core, from_chip, base, kv, factor, bias, grads, grads_in, lows, sums,
    ks, vs, seg, tenants,
    sem_w, sem_t, sem_q, sem_o, sem_p,
    s1, r1, s2, r2, s3, r3, s4, r4, s5, r5, s6, r6, s7, r7, sg, rg,
):
    chips = nten // 2
    rows_all, depth = tok.shape
    nb = rows_all // RB
    look = LONGEST // RB
    half = rows_all // 2
    kc = depth // KC
    d = lax.axis_index("dp")
    t = lax.axis_index("tensor")
    x = t // 2
    c = lax.rem(t, 2)
    other = 1 - c
    cf = c.astype(F32)
    partner = (d, 2 * x + other)
    peers = [(d, 2 * lax.rem(x + p, chips) + c) for p in range(1, chips)]
    groups = [lax.rem(d + i, ndp) for i in range(ndp)]

    def rows(b):
        return pl.ds(b * RB, RB)

    def load(src, dst, at, cols, sem):
        return pltpu.make_async_copy(src.at[at, cols], dst.at[at, cols], sem)

    loads = {}
    for b in range(nb):
        loads["q", b] = pltpu.make_async_copy(q_hbm.at[rows(b)], q.at[rows(b)], sem_q.at[b])
        loads["o", b] = pltpu.make_async_copy(o_hbm.at[rows(b)], o.at[rows(b)], sem_o.at[b])
    small = [
        pltpu.make_async_copy(src, dst, sem_p.at[i])
        for i, (src, dst) in enumerate(((ks_hbm, ks), (vs_hbm, vs), (seg_hbm, seg), (tenants_hbm, tenants)))]
    for copy in small:
        copy.start()
    for k in range(KC):
        kk = pl.ds(k * kc, kc)
        load(kw_hbm, kw, kk, slice(None), sem_w.at[k]).start()
        load(vw_hbm, vw, kk, slice(None), sem_w.at[KC + k]).start()
        load(tok_hbm, tok, pl.ds(0, half), kk, sem_t.at[k]).start()
    for k in range(KC):
        load(tok_hbm, tok, pl.ds(half, half), pl.ds(k * kc, kc), sem_t.at[KC + k]).start()
    for b in range(nb):
        loads["q", b].start()
        loads["o", b].start()

    barrier = pltpu.get_barrier_semaphore()
    count = 0
    for dev in [partner] + peers:
        pl.semaphore_signal(barrier, inc=1, device_id=dev, device_id_type=MESH)
        count += 1
    for i in range(1, ndp):
        for core in range(2):
            pl.semaphore_signal(barrier, inc=1, device_id=(groups[i], 2 * x + core), device_id_type=MESH)
            count += 1

    def send(src, dst, ssem, rsem, dev):
        copy = pltpu.make_async_remote_copy(
            src_ref=src, dst_ref=dst, send_sem=ssem, recv_sem=rsem, device_id=dev, device_id_type=MESH)
        copy.start()
        return copy

    def arrived(dst, rsem):
        pltpu.make_async_remote_copy(
            src_ref=dst, dst_ref=dst, send_sem=s1.at[0], recv_sem=rsem, device_id=partner, device_id_type=MESH
        ).wait_recv()

    sent = []

    for copy in small:
        copy.wait()
    segments = seg[...]
    counts = [jnp.sum(jnp.where(segments == s, 1.0, 0.0), axis=1, keepdims=True) for s in range(SEQS)]
    bounds = [jnp.zeros((1, 1), F32)]
    for s in range(SEQS):
        bounds.append(bounds[-1] + counts[s])
    start = jnp.zeros(segments.shape, F32)
    for s in range(1, SEQS):
        start = jnp.where(segments == s, bounds[s], start)
    own_cols = pl.ds(pl.multiple_of(x * HD, HD), HD)
    own_scale = ks[:, own_cols] * (1.0 - cf) + vs[:, own_cols] * cf
    tenant = lax.broadcasted_iota(jnp.int32, (NT, HD), 0)
    scale_rows = [
        jnp.sum(jnp.where(tenant == tenants[0, s], own_scale, 0.0), axis=0, keepdims=True) for s in range(SEQS)]

    def position(b):
        return lax.broadcasted_iota(jnp.int32, (RB, HD), 0).astype(F32) + float(b * RB)

    for b in range(nb):
        pos = position(b)
        f = jnp.broadcast_to(scale_rows[SEQS - 1], (RB, HD))
        for s in range(SEQS - 2, -1, -1):
            f = jnp.where(pos < bounds[s + 1], scale_rows[s], f)
        factor[rows(b), :] = f
        grads[0, rows(b), :] = jnp.zeros((RB, HD), F32)
        grads[1, rows(b), :] = jnp.zeros((RB, HD), F32)

    pl.semaphore_wait(barrier, count)

    def project(r, lo, hi):
        rr = pl.ds(r * half, half)

        def step(k, first):
            kk = pl.ds(pl.multiple_of(k * kc, kc), kc)
            if r == 0:
                load(kw_hbm, kw, kk, slice(None), sem_w.at[k]).wait()
                load(vw_hbm, vw, kk, slice(None), sem_w.at[KC + k]).wait()
            load(tok_hbm, tok, rr, kk, sem_t.at[r * KC + k]).wait()
            block = tok[rr, kk]
            for kind, weight in ((0, kw), (1, vw)):
                value = dot_nn(block, weight[kk, :])
                for h in range(chips):
                    piece = value[:, h * HD:(h + 1) * HD]
                    part[kind, h, rr, :] = piece if first else piece + part[kind, h, rr, :]

        if lo == 0:
            step(0, True)

        def more(k, _):
            step(k, False)
            return 0

        lax.fori_loop(max(lo, 1), hi, more, 0)

    def to_core(b):
        sent.append(send(part.at[other, :, rows(b)], from_core.at[:, rows(b)], s1.at[b], r1.at[b], partner))

    def to_chips(b):
        arrived(from_core.at[:, rows(b)], r1.at[b])
        for p in range(1, chips):
            j = lax.rem(x + p, chips)
            part[c, j, rows(b), :] = part[c, j, rows(b), :] + from_core[j, rows(b), :]
            i = (p - 1) * nb + b
            sent.append(send(part.at[c, j, rows(b)], from_chip.at[p - 1, rows(b)], s2.at[i], r2.at[i], peers[p - 1]))

    def finish(b):
        total = part[c, x, rows(b), :] + from_core[x, rows(b), :]
        for p in range(1, chips):
            arrived(from_chip.at[p - 1, rows(b)], r2.at[(p - 1) * nb + b])
            total = total + from_chip[p - 1, rows(b), :]
        base[rows(b), :] = total
        kv[c, rows(b), :] = (total * factor[rows(b), :]).astype(BF16)
        sent.append(send(kv.at[c, rows(b)], kv.at[c, rows(b)], s3.at[b], r3.at[b], partner))

    heads = q.shape[1] // HD
    score_scale = HD ** -0.5
    to_exp2 = score_scale * math.log2(math.e)

    def ready(b):
        arrived(kv.at[other, rows(b)], r3.at[b])
        loads["q", b].wait()
        loads["o", b].wait()
        first = max(0, b - look)
        query_pos = lax.broadcasted_iota(jnp.int32, (RB, RB), 1).astype(F32) + float(b * RB)
        begin = start[:, b * RB:(b + 1) * RB]
        for j in range(first, b + 1):
            key_pos = position(j)
            seen = (key_pos >= begin) & (key_pos <= query_pos)
            bias[rows(j - first), :] = jnp.where(seen, 0.0, -1e30)

    def attend(b, lo, hi):
        first = max(0, b - look)
        width = (b + 1 - first) * RB
        keys_at = pl.ds(first * RB, width)

        def several(i, _):
            cols = [pl.ds(pl.multiple_of((i * TOGETHER + n) * HD, HD), HD) for n in range(TOGETHER)]
            keys, values, hidden = kv[0, keys_at, :], kv[1, keys_at, :], bias[pl.ds(0, width), :]
            qs, outs, lows_, score_grads = [], [], [], []
            for col in cols:
                qh, oh = q[rows(b), col], o[rows(b), col]
                scores = dot_nt(keys, qh) + hidden
                grad = dot_nt(values, oh)
                peak = jnp.max(scores, axis=0, keepdims=True)
                e = jnp.exp2((scores - peak) * to_exp2)
                probs = e * (1.0 / jnp.sum(e, axis=0, keepdims=True))
                low = probs.astype(BF16)
                delta = jnp.sum(low.astype(F32) * grad, axis=0, keepdims=True)
                qs.append(qh)
                outs.append(oh)
                lows_.append(low)
                score_grads.append((probs * (grad - delta)).astype(BF16))
            grads[1, keys_at, :] = grads[1, keys_at, :] + dot_nn(
                jnp.concatenate(lows_, axis=1), jnp.concatenate(outs, axis=0))
            grads[0, keys_at, :] = grads[0, keys_at, :] + dot_nn(
                jnp.concatenate(score_grads, axis=1), jnp.concatenate(qs, axis=0))
            return 0

        lax.fori_loop(lo, hi, several, 0)

    def grads_to_core(b):
        sent.append(send(grads.at[other, rows(b)], grads_in.at[rows(b)], s4.at[b], r4.at[b], partner))

    tables = [jnp.zeros((1, HD), F32) for s in range(SEQS)]

    def lows_out(b):
        arrived(grads_in.at[rows(b)], r4.at[b])
        total = (grads[c, rows(b), :] + grads_in[rows(b), :]) * (cf + (1.0 - cf) * score_scale)
        lows[c, x, rows(b), :] = (total * factor[rows(b), :]).astype(BF16)
        for p in range(1, chips):
            i = (p - 1) * nb + b
            sent.append(send(lows.at[c, x, rows(b)], lows.at[c, x, rows(b)], s6.at[i], r6.at[i], peers[p - 1]))
        sent.append(send(lows.at[c, x, rows(b)], lows.at[c, x, rows(b)], s5.at[b], r5.at[b], partner))
        product = total * base[rows(b), :]
        pos = position(b)
        for s in range(SEQS):
            inside = (pos >= bounds[s]) & (pos < bounds[s + 1])
            tables[s] = tables[s] + jnp.sum(jnp.where(inside, product, 0.0), axis=0, keepdims=True)

    def forward(b):
        for p in range(1, chips):
            j = lax.rem(x + chips - p, chips)
            i = (p - 1) * nb + b
            arrived(lows.at[c, j, rows(b)], r6.at[i])
            sent.append(send(lows.at[c, j, rows(b)], lows.at[c, j, rows(b)], s7.at[i], r7.at[i], partner))

    project(0, 0, KC)
    for b in range(nb // 2):
        to_core(b)
    project(1, 0, KC // 2)
    for b in range(nb // 2):
        to_chips(b)
    project(1, KC // 2, KC)
    for b in range(nb // 2, nb):
        to_core(b)
    for b in range(nb // 2, nb):
        to_chips(b)
    finish(0)
    finish(1)
    pairs = heads // TOGETHER
    for b in range(nb):
        ready(b)
        last = b == nb - 1
        attend(b, 0, pairs // 2 if last else pairs)
        if b + 2 < nb:
            finish(b + 2)
        if last:
            for j in range(nb - 1 - look):
                lows_out(j)
            attend(b, pairs // 2, pairs)
        elif b >= look:
            grads_to_core(b - look)
    for j in range(nb - 1 - look, nb):
        grads_to_core(j)
    for j in range(nb - 1 - look, nb):
        lows_out(j)

    for s in range(SEQS):
        sums[0, c, pl.ds(s, 1), :] = tables[s]
        sums[0, c, pl.ds(SEQS + s, 1), :] = jnp.full((1, HD), 1.0, F32) * tenants[0, s].astype(F32)
    for i in range(ndp):
        if i == 0:
            sent.append(send(sums.at[0, c], sums.at[0, c], sg.at[other], rg.at[c], partner))
        else:
            for core in range(2):
                sent.append(send(
                    sums.at[0, c], sums.at[i, c], sg.at[2 * i + core], rg.at[2 * i + c], (groups[i], 2 * x + core)))
    for b in range(nb):
        forward(b)
    for b in range(nb):
        arrived(lows.at[other, x, rows(b)], r5.at[b])
        for p in range(1, chips):
            j = lax.rem(x + chips - p, chips)
            arrived(lows.at[other, j, rows(b)], r7.at[(p - 1) * nb + b])
    for kind in range(2):
        for h in range(chips):
            low_out[:, pl.ds((kind * chips + h) * HD, HD)] = lows[kind, h]
    for i in range(ndp):
        if i == 0:
            arrived(sums.at[0, other], rg.at[other])
        else:
            for core in range(2):
                arrived(sums.at[i, core], rg.at[2 * i + core])
    for i in range(ndp):
        for core in range(2):
            value = sums[i, core]
            turned = jnp.concatenate([value[:, HD // 2:], value[:, :HD // 2]], axis=1)
            sums_out[i, core] = value * (1.0 - cf) + turned * cf
    for copy in sent:
        copy.wait_send()


def closing(ndp, low, kw, vw, sums, grad_out, key_out, value_out):
    weights = jnp.concatenate([kw[...], vw[...]], axis=1)
    grad_out[...] = dot_nt(low[...], weights).astype(BF16)

    @pl.when(pl.program_id(0) == 0)
    def _():
        tenant = lax.broadcasted_iota(jnp.int32, (NT, HD), 0).astype(F32)
        for kind, out in ((0, key_out), (1, value_out)):
            total = jnp.zeros((NT, HD), F32)
            for i in range(ndp):
                block = sums[i, kind]
                for s in range(SEQS):
                    total = total + jnp.where(tenant == block[SEQS + s:SEQS + s + 1, :], block[s:s + 1, :], 0.0)
            out[...] = total[:, :HD // 2]


def on_device(ndp, nten, tokens, queries, out_grad, key_weight, value_weight, key_scale, value_scale, segment_ids, tenant_ids):
    chips = nten // 2
    rows_all, depth = tokens.shape
    nb = rows_all // RB
    wide = key_weight.shape[1]
    hbm = pl.BlockSpec(memory_space=pltpu.HBM)
    vmem = pl.BlockSpec(memory_space=pltpu.VMEM)
    sem = pltpu.SemaphoreType.DMA
    many = max(1, (chips - 1) * nb)
    low, sums = pl.pallas_call(
        functools.partial(inner, ndp, nten),
        out_shape=(
            jax.ShapeDtypeStruct((rows_all, 2 * wide), BF16),
            jax.ShapeDtypeStruct((ndp, 2, 2 * SEQS, HD), F32),
        ),
        in_specs=[hbm] * 9,
        out_specs=(vmem, vmem),
        scratch_shapes=[
            pltpu.VMEM(tokens.shape, BF16),
            pltpu.VMEM(queries.shape, BF16),
            pltpu.VMEM(out_grad.shape, BF16),
            pltpu.VMEM(key_weight.shape, BF16),
            pltpu.VMEM(value_weight.shape, BF16),
            pltpu.VMEM((2, chips, rows_all, HD), F32),
            pltpu.VMEM((chips, rows_all, HD), F32),
            pltpu.VMEM((max(1, chips - 1), rows_all, HD), F32),
            pltpu.VMEM((rows_all, HD), F32),
            pltpu.VMEM((2, rows_all, HD), BF16),
            pltpu.VMEM((rows_all, HD), F32),
            pltpu.VMEM((LONGEST + RB, RB), F32),
            pltpu.VMEM((2, rows_all, HD), F32),
            pltpu.VMEM((rows_all, HD), F32),
            pltpu.VMEM((2, chips, rows_all, HD), BF16),
            pltpu.VMEM((ndp, 2, 2 * SEQS, HD), F32),
            pltpu.VMEM(key_scale.shape, F32),
            pltpu.VMEM(value_scale.shape, F32),
            pltpu.VMEM(segment_ids.shape, jnp.int32),
            pltpu.SMEM(tenant_ids.shape, jnp.int32),
            sem((2 * KC,)), sem((2 * KC,)), sem((nb,)), sem((nb,)), sem((4,)),
            sem((nb,)), sem((nb,)), sem((many,)), sem((many,)), sem((nb,)), sem((nb,)), sem((nb,)), sem((nb,)),
            sem((nb,)), sem((nb,)), sem((many,)), sem((many,)), sem((many,)), sem((many,)),
            sem((2 * ndp,)), sem((2 * ndp,)),
        ],
        compiler_params=pltpu.CompilerParams(
            collective_id=0, has_side_effects=True, vmem_limit_bytes=VMEM_LIMIT),
    )(tokens, queries, out_grad, key_weight, value_weight, key_scale, value_scale, segment_ids, tenant_ids)

    block = min(512, depth)
    return pl.pallas_call(
        functools.partial(closing, ndp),
        grid=(depth // block,),
        out_shape=(
            jax.ShapeDtypeStruct((rows_all, depth), BF16),
            jax.ShapeDtypeStruct((NT, HD // 2), F32),
            jax.ShapeDtypeStruct((NT, HD // 2), F32),
        ),
        in_specs=[
            pl.BlockSpec((rows_all, 2 * wide), lambda i: (0, 0)),
            pl.BlockSpec((block, wide), lambda i: (i, 0)),
            pl.BlockSpec((block, wide), lambda i: (i, 0)),
            pl.BlockSpec((ndp, 2, 2 * SEQS, HD), lambda i: (0, 0, 0, 0)),
        ],
        out_specs=(
            pl.BlockSpec((rows_all, block), lambda i: (0, i)),
            pl.BlockSpec((NT, HD // 2), lambda i: (0, 0)),
            pl.BlockSpec((NT, HD // 2), lambda i: (0, 0)),
        ),
        compiler_params=pltpu.CompilerParams(vmem_limit_bytes=VMEM_LIMIT),
    )(low, key_weight, value_weight, sums)


def solution(mesh):
    return jax.shard_map(
        functools.partial(on_device, mesh.shape["dp"], mesh.shape["tensor"]),
        mesh=mesh,
        in_specs=(
            P("dp", "tensor"),
            P("dp", "tensor"),
            P("dp", "tensor"),
            P("tensor", None),
            P("tensor", None),
            P(),
            P(),
            P("dp", None),
            P("dp", None),
        ),
        out_specs=(P("dp", "tensor"), P(None, "tensor"), P(None, "tensor")),
        check_vma=False,
    )
```

```python
import functools
import math

import jax
import jax.numpy as jnp
from jax import lax
from jax.experimental import pallas as pl
from jax.experimental.pallas import tpu as pltpu
from jax.sharding import PartitionSpec as P

MESH = pl.DeviceIdType.MESH
F32 = jnp.float32
BF16 = jnp.bfloat16
SEQS = 4
NT = 32
HD = 128
RB = 128
LONGEST = 256
VMEM_LIMIT = 64 * 1024 * 1024
TOGETHER = 4
FB = 512
KC = 4


def dot_nt(a, b):
    return lax.dot_general(a, b, (((1,), (1,)), ((), ())), preferred_element_type=F32)


def dot_nn(a, b):
    return jnp.dot(a, b, preferred_element_type=F32)


def inner(
    ndp, nten, tok_hbm, q_hbm, o_hbm, kw_hbm, vw_hbm, ks_hbm, vs_hbm, seg_hbm, tenants_hbm,
    low_out, sums_out,
    tok, q, o, kw, vw, part, from_core, from_chip, base, kv, factor, bias, grads, grads_in, lows, sums,
    ks, vs, seg, tenants,
    sem_w, sem_t, sem_q, sem_o, sem_p, sem_s,
    s1, r1, s2, r2, s3, r3, s4, r4, s5, r5, s6, r6, s7, r7, sg, rg,
):
    chips = nten // 2
    rows_all, depth = tok.shape
    nb = rows_all // RB
    look = LONGEST // RB
    half = rows_all // 2
    kc = depth // KC
    d = lax.axis_index("dp")
    t = lax.axis_index("tensor")
    x = t // 2
    c = lax.rem(t, 2)
    other = 1 - c
    cf = c.astype(F32)
    partner = (d, 2 * x + other)
    peers = [(d, 2 * lax.rem(x + p, chips) + c) for p in range(1, chips)]
    groups = [lax.rem(d + i, ndp) for i in range(ndp)]

    def rows(b):
        return pl.ds(b * RB, RB)

    def load(src, dst, at, cols, sem):
        return pltpu.make_async_copy(src.at[at, cols], dst.at[at, cols], sem)

    loads = {}
    for b in range(nb):
        loads["q", b] = pltpu.make_async_copy(q_hbm.at[rows(b)], q.at[rows(b)], sem_q.at[b])
        loads["o", b] = pltpu.make_async_copy(o_hbm.at[rows(b)], o.at[rows(b)], sem_o.at[b])
    small = [
        pltpu.make_async_copy(src, dst, sem_p.at[i])
        for i, (src, dst) in enumerate(((ks_hbm, ks), (vs_hbm, vs), (seg_hbm, seg), (tenants_hbm, tenants)))]
    for copy in small:
        copy.start()
    for k in range(KC):
        kk = pl.ds(k * kc, kc)
        load(kw_hbm, kw, kk, slice(None), sem_w.at[k]).start()
        load(vw_hbm, vw, kk, slice(None), sem_w.at[KC + k]).start()
        load(tok_hbm, tok, pl.ds(0, half), kk, sem_t.at[k]).start()
    for k in range(KC):
        load(tok_hbm, tok, pl.ds(half, half), pl.ds(k * kc, kc), sem_t.at[KC + k]).start()
    for b in range(nb):
        loads["q", b].start()
        loads["o", b].start()

    barrier = pltpu.get_barrier_semaphore()
    count = 0
    for dev in [partner] + peers:
        pl.semaphore_signal(barrier, inc=1, device_id=dev, device_id_type=MESH)
        count += 1
    for i in range(1, ndp):
        for core in range(2):
            pl.semaphore_signal(barrier, inc=1, device_id=(groups[i], 2 * x + core), device_id_type=MESH)
            count += 1

    def send(src, dst, ssem, rsem, dev):
        copy = pltpu.make_async_remote_copy(
            src_ref=src, dst_ref=dst, send_sem=ssem, recv_sem=rsem, device_id=dev, device_id_type=MESH)
        copy.start()
        return copy

    def arrived(dst, rsem):
        pltpu.make_async_remote_copy(
            src_ref=dst, dst_ref=dst, send_sem=s1.at[0], recv_sem=rsem, device_id=partner, device_id_type=MESH
        ).wait_recv()

    sent = []

    def project(r, lo, hi):
        rr = pl.ds(r * half, half)

        def step(k, first):
            kk = pl.ds(pl.multiple_of(k * kc, kc), kc)
            if r == 0:
                load(kw_hbm, kw, kk, slice(None), sem_w.at[k]).wait()
                load(vw_hbm, vw, kk, slice(None), sem_w.at[KC + k]).wait()
            load(tok_hbm, tok, rr, kk, sem_t.at[r * KC + k]).wait()
            block = tok[rr, kk]
            for kind, weight in ((0, kw), (1, vw)):
                value = dot_nn(block, weight[kk, :])
                for h in range(chips):
                    piece = value[:, h * HD:(h + 1) * HD]
                    part[kind, h, rr, :] = piece if first else piece + part[kind, h, rr, :]

        if lo == 0:
            step(0, True)

        def more(k, _):
            step(k, False)
            return 0

        lax.fori_loop(max(lo, 1), hi, more, 0)

    def to_core(b):
        sent.append(send(part.at[other, :, rows(b)], from_core.at[:, rows(b)], s1.at[b], r1.at[b], partner))

    def to_chips(b):
        arrived(from_core.at[:, rows(b)], r1.at[b])
        for p in range(1, chips):
            j = lax.rem(x + p, chips)
            part[c, j, rows(b), :] = part[c, j, rows(b), :] + from_core[j, rows(b), :]
            i = (p - 1) * nb + b
            sent.append(send(part.at[c, j, rows(b)], from_chip.at[p - 1, rows(b)], s2.at[i], r2.at[i], peers[p - 1]))

    def position(b):
        return lax.broadcasted_iota(jnp.int32, (RB, HD), 0).astype(F32) + float(b * RB)

    def finish(b):
        total = part[c, x, rows(b), :] + from_core[x, rows(b), :]
        for p in range(1, chips):
            arrived(from_chip.at[p - 1, rows(b)], r2.at[(p - 1) * nb + b])
            total = total + from_chip[p - 1, rows(b), :]
        base[rows(b), :] = total
        kv[c, rows(b), :] = (total * factor[rows(b), :]).astype(BF16)
        sent.append(send(kv.at[c, rows(b)], kv.at[c, rows(b)], s3.at[b], r3.at[b], partner))

    heads = q.shape[1] // HD
    score_scale = HD ** -0.5
    to_exp2 = score_scale * math.log2(math.e)

    def ready(b):
        arrived(kv.at[other, rows(b)], r3.at[b])
        loads["q", b].wait()
        loads["o", b].wait()
        first = max(0, b - look)
        query_pos = lax.broadcasted_iota(jnp.int32, (RB, RB), 1).astype(F32) + float(b * RB)
        begin = start[:, b * RB:(b + 1) * RB]
        for j in range(first, b + 1):
            key_pos = position(j)
            seen = (key_pos >= begin) & (key_pos <= query_pos)
            bias[rows(j - first), :] = jnp.where(seen, 0.0, -1e30)

    def attend(b, lo, hi):
        first = max(0, b - look)
        width = (b + 1 - first) * RB
        keys_at = pl.ds(first * RB, width)

        def several(i, _):
            cols = [pl.ds(pl.multiple_of((i * TOGETHER + n) * HD, HD), HD) for n in range(TOGETHER)]
            keys, values, hidden = kv[0, keys_at, :], kv[1, keys_at, :], bias[pl.ds(0, width), :]
            qs, outs, lows_, score_grads = [], [], [], []
            for col in cols:
                qh, oh = q[rows(b), col], o[rows(b), col]
                scores = dot_nt(keys, qh) + hidden
                grad = dot_nt(values, oh)
                peak = jnp.max(scores, axis=0, keepdims=True)
                e = jnp.exp2((scores - peak) * to_exp2)
                probs = e * (1.0 / jnp.sum(e, axis=0, keepdims=True))
                low = probs.astype(BF16)
                delta = jnp.sum(low.astype(F32) * grad, axis=0, keepdims=True)
                qs.append(qh)
                outs.append(oh)
                lows_.append(low)
                score_grads.append((probs * (grad - delta)).astype(BF16))
            grads[1, keys_at, :] = grads[1, keys_at, :] + dot_nn(
                jnp.concatenate(lows_, axis=1), jnp.concatenate(outs, axis=0))
            grads[0, keys_at, :] = grads[0, keys_at, :] + dot_nn(
                jnp.concatenate(score_grads, axis=1), jnp.concatenate(qs, axis=0))
            return 0

        lax.fori_loop(lo, hi, several, 0)

    def grads_to_core(b):
        sent.append(send(grads.at[other, rows(b)], grads_in.at[rows(b)], s4.at[b], r4.at[b], partner))

    tables = [jnp.zeros((1, HD), F32) for s in range(SEQS)]

    def lows_out(b):
        arrived(grads_in.at[rows(b)], r4.at[b])
        total = (grads[c, rows(b), :] + grads_in[rows(b), :]) * (cf + (1.0 - cf) * score_scale)
        lows[c, x, rows(b), :] = (total * factor[rows(b), :]).astype(BF16)
        for p in range(1, chips):
            i = (p - 1) * nb + b
            sent.append(send(lows.at[c, x, rows(b)], lows.at[c, x, rows(b)], s6.at[i], r6.at[i], peers[p - 1]))
        sent.append(send(lows.at[c, x, rows(b)], lows.at[c, x, rows(b)], s5.at[b], r5.at[b], partner))
        product = total * base[rows(b), :]
        pos = position(b)
        for s in range(SEQS):
            inside = (pos >= bounds[s]) & (pos < bounds[s + 1])
            tables[s] = tables[s] + jnp.sum(jnp.where(inside, product, 0.0), axis=0, keepdims=True)

    def forward(b):
        for p in range(1, chips):
            j = lax.rem(x + chips - p, chips)
            i = (p - 1) * nb + b
            arrived(lows.at[c, j, rows(b)], r6.at[i])
            sent.append(send(lows.at[c, j, rows(b)], lows.at[c, j, rows(b)], s7.at[i], r7.at[i], partner))

    project(0, 0, KC)
    pl.semaphore_wait(barrier, count)
    for b in range(nb // 2):
        to_core(b)
    for copy in small:
        copy.wait()
    segments = seg[...]
    counts = [jnp.sum(jnp.where(segments == s, 1.0, 0.0), axis=1, keepdims=True) for s in range(SEQS)]
    bounds = [jnp.zeros((1, 1), F32)]
    for s in range(SEQS):
        bounds.append(bounds[-1] + counts[s])
    start = jnp.zeros(segments.shape, F32)
    for s in range(1, SEQS):
        start = jnp.where(segments == s, bounds[s], start)
    own_cols = pl.ds(pl.multiple_of(x * HD, HD), HD)
    own_scale = ks[:, own_cols] * (1.0 - cf) + vs[:, own_cols] * cf
    tenant = lax.broadcasted_iota(jnp.int32, (NT, HD), 0)
    scale_rows = [
        jnp.sum(jnp.where(tenant == tenants[0, s], own_scale, 0.0), axis=0, keepdims=True) for s in range(SEQS)]

    for b in range(nb):
        pos = position(b)
        f = jnp.broadcast_to(scale_rows[SEQS - 1], (RB, HD))
        for s in range(SEQS - 2, -1, -1):
            f = jnp.where(pos < bounds[s + 1], scale_rows[s], f)
        factor[rows(b), :] = f
        grads[0, rows(b), :] = jnp.zeros((RB, HD), F32)
        grads[1, rows(b), :] = jnp.zeros((RB, HD), F32)
    project(1, 0, KC // 2)
    for b in range(nb // 2):
        to_chips(b)
    project(1, KC // 2, KC)
    for b in range(nb // 2, nb):
        to_core(b)
    for b in range(nb // 2, nb):
        to_chips(b)
    finish(0)
    finish(1)
    pairs = heads // TOGETHER
    for b in range(nb):
        ready(b)
        last = b == nb - 1
        attend(b, 0, pairs // 2 if last else pairs)
        if b + 2 < nb:
            finish(b + 2)
        if last:
            for j in range(nb - 1 - look):
                lows_out(j)
            attend(b, pairs // 2, pairs)
        elif b >= look:
            grads_to_core(b - look)
    for j in range(nb - 1 - look, nb):
        grads_to_core(j)
    for j in range(nb - 1 - look, nb):
        lows_out(j)

    for s in range(SEQS):
        sums[0, c, pl.ds(s, 1), :] = tables[s]
        sums[0, c, pl.ds(SEQS + s, 1), :] = jnp.full((1, HD), 1.0, F32) * tenants[0, s].astype(F32)
    for i in range(ndp):
        if i == 0:
            sent.append(send(sums.at[0, c], sums.at[0, c], sg.at[other], rg.at[c], partner))
        else:
            for core in range(2):
                sent.append(send(
                    sums.at[0, c], sums.at[i, c], sg.at[2 * i + core], rg.at[2 * i + c], (groups[i], 2 * x + core)))
    for b in range(nb):
        forward(b)
    for b in range(nb):
        arrived(lows.at[other, x, rows(b)], r5.at[b])
        for p in range(1, chips):
            j = lax.rem(x + chips - p, chips)
            arrived(lows.at[other, j, rows(b)], r7.at[(p - 1) * nb + b])
    saves = []
    for kind in range(2):
        for h in range(chips):
            n = kind * chips + h
            saves.append(pltpu.make_async_copy(lows.at[kind, h], low_out.at[:, pl.ds(n * HD, HD)], sem_s.at[n]))
            saves[-1].start()
    for i in range(ndp):
        if i == 0:
            arrived(sums.at[0, other], rg.at[other])
        else:
            for core in range(2):
                arrived(sums.at[i, core], rg.at[2 * i + core])
    for i in range(ndp):
        for core in range(2):
            value = sums[i, core]
            turned = jnp.concatenate([value[:, HD // 2:], value[:, :HD // 2]], axis=1)
            sums_out[i, core] = value * (1.0 - cf) + turned * cf
    for copy in saves:
        copy.wait()
    for copy in sent:
        copy.wait_send()


def closing(
    ndp, low_hbm, kw_hbm, vw_hbm, sums, grad_hbm, key_out, value_out, low, kw, vw, grad, sem_l, sem_k, sem_v, sem_g
):
    depth = kw.shape[0]
    block = min(FB, depth)
    count = depth // block

    def load_low():
        return pltpu.make_async_copy(low_hbm, low, sem_l.at[0])

    def at(i):
        return pl.ds(pl.multiple_of(i * block, block), block)

    def load_key(i):
        return pltpu.make_async_copy(kw_hbm.at[at(i)], kw.at[at(i)], sem_k.at[i])

    def load_value(i):
        return pltpu.make_async_copy(vw_hbm.at[at(i)], vw.at[at(i)], sem_v.at[i])

    def save(i):
        return pltpu.make_async_copy(grad.at[:, at(i)], grad_hbm.at[:, at(i)], sem_g.at[i])

    load_low().start()
    for i in range(count):
        load_key(i).start()
        load_value(i).start()
    load_low().wait()

    def step(i, _):
        load_key(i).wait()
        load_value(i).wait()
        weights = jnp.concatenate([kw[at(i), :], vw[at(i), :]], axis=1)
        grad[:, at(i)] = dot_nt(low[...], weights).astype(BF16)
        save(i).start()
        return 0

    lax.fori_loop(0, count, step, 0)

    tenant = lax.broadcasted_iota(jnp.int32, (NT, HD), 0).astype(F32)
    for kind, out in ((0, key_out), (1, value_out)):
        total = jnp.zeros((NT, HD), F32)
        for i in range(ndp):
            rows = sums[i, kind]
            for s in range(SEQS):
                total = total + jnp.where(tenant == rows[SEQS + s:SEQS + s + 1, :], rows[s:s + 1, :], 0.0)
        out[...] = total[:, :HD // 2]
    for i in range(count):
        save(i).wait()


def on_device(ndp, nten, tokens, queries, out_grad, key_weight, value_weight, key_scale, value_scale, segment_ids, tenant_ids):
    chips = nten // 2
    rows_all, depth = tokens.shape
    nb = rows_all // RB
    wide = key_weight.shape[1]
    hbm = pl.BlockSpec(memory_space=pltpu.HBM)
    vmem = pl.BlockSpec(memory_space=pltpu.VMEM)
    sem = pltpu.SemaphoreType.DMA
    many = max(1, (chips - 1) * nb)
    low, sums = pl.pallas_call(
        functools.partial(inner, ndp, nten),
        out_shape=(
            jax.ShapeDtypeStruct((rows_all, 2 * wide), BF16),
            jax.ShapeDtypeStruct((ndp, 2, 2 * SEQS, HD), F32),
        ),
        in_specs=[hbm] * 9,
        out_specs=(hbm, vmem),
        scratch_shapes=[
            pltpu.VMEM(tokens.shape, BF16),
            pltpu.VMEM(queries.shape, BF16),
            pltpu.VMEM(out_grad.shape, BF16),
            pltpu.VMEM(key_weight.shape, BF16),
            pltpu.VMEM(value_weight.shape, BF16),
            pltpu.VMEM((2, chips, rows_all, HD), F32),
            pltpu.VMEM((chips, rows_all, HD), F32),
            pltpu.VMEM((max(1, chips - 1), rows_all, HD), F32),
            pltpu.VMEM((rows_all, HD), F32),
            pltpu.VMEM((2, rows_all, HD), BF16),
            pltpu.VMEM((rows_all, HD), F32),
            pltpu.VMEM((LONGEST + RB, RB), F32),
            pltpu.VMEM((2, rows_all, HD), F32),
            pltpu.VMEM((rows_all, HD), F32),
            pltpu.VMEM((2, chips, rows_all, HD), BF16),
            pltpu.VMEM((ndp, 2, 2 * SEQS, HD), F32),
            pltpu.VMEM(key_scale.shape, F32),
            pltpu.VMEM(value_scale.shape, F32),
            pltpu.VMEM(segment_ids.shape, jnp.int32),
            pltpu.SMEM(tenant_ids.shape, jnp.int32),
            sem((2 * KC,)), sem((2 * KC,)), sem((nb,)), sem((nb,)), sem((4,)), sem((2 * chips,)),
            sem((nb,)), sem((nb,)), sem((many,)), sem((many,)), sem((nb,)), sem((nb,)), sem((nb,)), sem((nb,)),
            sem((nb,)), sem((nb,)), sem((many,)), sem((many,)), sem((many,)), sem((many,)),
            sem((2 * ndp,)), sem((2 * ndp,)),
        ],
        compiler_params=pltpu.CompilerParams(
            collective_id=0, has_side_effects=True, vmem_limit_bytes=VMEM_LIMIT),
    )(tokens, queries, out_grad, key_weight, value_weight, key_scale, value_scale, segment_ids, tenant_ids)

    count = depth // min(FB, depth)
    return pl.pallas_call(
        functools.partial(closing, ndp),
        out_shape=(
            jax.ShapeDtypeStruct((rows_all, depth), BF16),
            jax.ShapeDtypeStruct((NT, HD // 2), F32),
            jax.ShapeDtypeStruct((NT, HD // 2), F32),
        ),
        in_specs=[hbm] * 3 + [vmem],
        out_specs=(hbm, vmem, vmem),
        scratch_shapes=[
            pltpu.VMEM((rows_all, 2 * wide), BF16),
            pltpu.VMEM(key_weight.shape, BF16),
            pltpu.VMEM(value_weight.shape, BF16),
            pltpu.VMEM((rows_all, depth), BF16),
            sem((1,)), sem((count,)), sem((count,)), sem((count,)),
        ],
        compiler_params=pltpu.CompilerParams(vmem_limit_bytes=VMEM_LIMIT),
    )(low, key_weight, value_weight, sums)


def solution(mesh):
    return jax.shard_map(
        functools.partial(on_device, mesh.shape["dp"], mesh.shape["tensor"]),
        mesh=mesh,
        in_specs=(
            P("dp", "tensor"),
            P("dp", "tensor"),
            P("dp", "tensor"),
            P("tensor", None),
            P("tensor", None),
            P(),
            P(),
            P("dp", None),
            P("dp", None),
        ),
        out_specs=(P("dp", "tensor"), P(None, "tensor"), P(None, "tensor")),
        check_vma=False,
    )
```

```python
import functools
import math

import jax
import jax.numpy as jnp
from jax import lax
from jax.experimental import pallas as pl
from jax.experimental.pallas import tpu as pltpu
from jax.sharding import PartitionSpec as P

MESH = pl.DeviceIdType.MESH
F32 = jnp.float32
BF16 = jnp.bfloat16
SEQS = 4
NT = 32
HD = 128
RB = 128
LONGEST = 256
VMEM_LIMIT = 64 * 1024 * 1024
TOGETHER = 4
FB = 512
KD = 512


def dot_nt(a, b):
    return lax.dot_general(a, b, (((1,), (1,)), ((), ())), preferred_element_type=F32)


def dot_nn(a, b):
    return jnp.dot(a, b, preferred_element_type=F32)


def inner(
    ndp, nten, tok_hbm, q_hbm, o_hbm, kw_hbm, vw_hbm, ks_hbm, vs_hbm, seg_hbm, tenants_hbm,
    low_out, sums_out,
    tok, q, o, kw, vw, part, from_core, from_chip, base, kv, factor, bias, grads, grads_in, lows, sums,
    ks, vs, seg, tenants,
    sem_w, sem_t, sem_q, sem_o, sem_p, sem_s,
    s1, r1, s2, r2, s3, r3, s4, r4, s5, r5, s6, r6, s7, r7, sg, rg,
):
    chips = nten // 2
    rows_all, depth = tok.shape
    nb = rows_all // RB
    look = LONGEST // RB
    kc = min(KD, depth)
    pieces = depth // kc
    d = lax.axis_index("dp")
    t = lax.axis_index("tensor")
    x = t // 2
    c = lax.rem(t, 2)
    other = 1 - c
    cf = c.astype(F32)
    partner = (d, 2 * x + other)
    peers = [(d, 2 * lax.rem(x + p, chips) + c) for p in range(1, chips)]
    groups = [lax.rem(d + i, ndp) for i in range(ndp)]

    def rows(b):
        return pl.ds(b * RB, RB)

    def load(src, dst, at, cols, sem):
        return pltpu.make_async_copy(src.at[at, cols], dst.at[at, cols], sem)

    loads = {}
    for b in range(nb):
        loads["q", b] = pltpu.make_async_copy(q_hbm.at[rows(b)], q.at[rows(b)], sem_q.at[b])
        loads["o", b] = pltpu.make_async_copy(o_hbm.at[rows(b)], o.at[rows(b)], sem_o.at[b])
    small = [
        pltpu.make_async_copy(src, dst, sem_p.at[i])
        for i, (src, dst) in enumerate(((ks_hbm, ks), (vs_hbm, vs), (seg_hbm, seg), (tenants_hbm, tenants)))]
    for copy in small:
        copy.start()
    for k in range(pieces):
        kk = pl.ds(k * kc, kc)
        load(kw_hbm, kw, kk, slice(None), sem_w.at[k]).start()
        load(vw_hbm, vw, kk, slice(None), sem_w.at[pieces + k]).start()
        load(tok_hbm, tok, slice(None), kk, sem_t.at[k]).start()
    for b in range(nb):
        loads["q", b].start()
        loads["o", b].start()

    barrier = pltpu.get_barrier_semaphore()
    count = 0
    for dev in [partner] + peers:
        pl.semaphore_signal(barrier, inc=1, device_id=dev, device_id_type=MESH)
        count += 1
    for i in range(1, ndp):
        for core in range(2):
            pl.semaphore_signal(barrier, inc=1, device_id=(groups[i], 2 * x + core), device_id_type=MESH)
            count += 1

    def send(src, dst, ssem, rsem, dev):
        copy = pltpu.make_async_remote_copy(
            src_ref=src, dst_ref=dst, send_sem=ssem, recv_sem=rsem, device_id=dev, device_id_type=MESH)
        copy.start()
        return copy

    def arrived(dst, rsem):
        pltpu.make_async_remote_copy(
            src_ref=dst, dst_ref=dst, send_sem=s1.at[0], recv_sem=rsem, device_id=partner, device_id_type=MESH
        ).wait_recv()

    sent = []

    def project():
        deep = kc // 2

        def step(k, first):
            kk = pl.ds(pl.multiple_of(k * kc, kc), kc)
            load(kw_hbm, kw, kk, slice(None), sem_w.at[k]).wait()
            load(vw_hbm, vw, kk, slice(None), sem_w.at[pieces + k]).wait()
            load(tok_hbm, tok, slice(None), kk, sem_t.at[k]).wait()
            value = None
            for n in range(2):
                at = pl.ds(pl.multiple_of(k * kc + n * deep, deep), deep)
                weights = jnp.concatenate([kw[at, :], vw[at, :]], axis=1)
                term = dot_nn(tok[:, at], weights)
                value = term if value is None else value + term
            for kind in range(2):
                for h in range(chips):
                    n = kind * chips + h
                    piece = value[:, n * HD:(n + 1) * HD]
                    part[kind, h] = piece if first else piece + part[kind, h]

        step(0, True)

        def more(k, _):
            step(k, False)
            return 0

        lax.fori_loop(1, pieces, more, 0)

    def to_core(b):
        sent.append(send(part.at[other, :, rows(b)], from_core.at[:, rows(b)], s1.at[b], r1.at[b], partner))

    def to_chips(b):
        arrived(from_core.at[:, rows(b)], r1.at[b])
        for p in range(1, chips):
            j = lax.rem(x + p, chips)
            part[c, j, rows(b), :] = part[c, j, rows(b), :] + from_core[j, rows(b), :]
            i = (p - 1) * nb + b
            sent.append(send(part.at[c, j, rows(b)], from_chip.at[p - 1, rows(b)], s2.at[i], r2.at[i], peers[p - 1]))

    def position(b):
        return lax.broadcasted_iota(jnp.int32, (RB, HD), 0).astype(F32) + float(b * RB)

    def finish(b):
        total = part[c, x, rows(b), :] + from_core[x, rows(b), :]
        for p in range(1, chips):
            arrived(from_chip.at[p - 1, rows(b)], r2.at[(p - 1) * nb + b])
            total = total + from_chip[p - 1, rows(b), :]
        base[rows(b), :] = total
        kv[c, rows(b), :] = (total * factor[rows(b), :]).astype(BF16)
        sent.append(send(kv.at[c, rows(b)], kv.at[c, rows(b)], s3.at[b], r3.at[b], partner))

    heads = q.shape[1] // HD
    score_scale = HD ** -0.5
    to_exp2 = score_scale * math.log2(math.e)

    def ready(b):
        arrived(kv.at[other, rows(b)], r3.at[b])
        loads["q", b].wait()
        loads["o", b].wait()
        first = max(0, b - look)
        query_pos = lax.broadcasted_iota(jnp.int32, (RB, RB), 1).astype(F32) + float(b * RB)
        begin = start[:, b * RB:(b + 1) * RB]
        for j in range(first, b + 1):
            key_pos = position(j)
            seen = (key_pos >= begin) & (key_pos <= query_pos)
            bias[rows(j - first), :] = jnp.where(seen, 0.0, -1e30)

    def attend(b, lo, hi):
        first = max(0, b - look)
        width = (b + 1 - first) * RB
        keys_at = pl.ds(first * RB, width)

        def several(i, _):
            cols = [pl.ds(pl.multiple_of((i * TOGETHER + n) * HD, HD), HD) for n in range(TOGETHER)]
            keys, values, hidden = kv[0, keys_at, :], kv[1, keys_at, :], bias[pl.ds(0, width), :]
            qs, outs, lows_, score_grads = [], [], [], []
            for col in cols:
                qh, oh = q[rows(b), col], o[rows(b), col]
                scores = dot_nt(keys, qh) + hidden
                grad = dot_nt(values, oh)
                peak = jnp.max(scores, axis=0, keepdims=True)
                e = jnp.exp2((scores - peak) * to_exp2)
                probs = e * (1.0 / jnp.sum(e, axis=0, keepdims=True))
                low = probs.astype(BF16)
                delta = jnp.sum(low.astype(F32) * grad, axis=0, keepdims=True)
                qs.append(qh)
                outs.append(oh)
                lows_.append(low)
                score_grads.append((probs * (grad - delta)).astype(BF16))
            grads[1, keys_at, :] = grads[1, keys_at, :] + dot_nn(
                jnp.concatenate(lows_, axis=1), jnp.concatenate(outs, axis=0))
            grads[0, keys_at, :] = grads[0, keys_at, :] + dot_nn(
                jnp.concatenate(score_grads, axis=1), jnp.concatenate(qs, axis=0))
            return 0

        lax.fori_loop(lo, hi, several, 0)

    def grads_to_core(b):
        sent.append(send(grads.at[other, rows(b)], grads_in.at[rows(b)], s4.at[b], r4.at[b], partner))

    tables = [jnp.zeros((1, HD), F32) for s in range(SEQS)]

    def lows_out(b):
        arrived(grads_in.at[rows(b)], r4.at[b])
        total = (grads[c, rows(b), :] + grads_in[rows(b), :]) * (cf + (1.0 - cf) * score_scale)
        lows[c, x, rows(b), :] = (total * factor[rows(b), :]).astype(BF16)
        for p in range(1, chips):
            i = (p - 1) * nb + b
            sent.append(send(lows.at[c, x, rows(b)], lows.at[c, x, rows(b)], s6.at[i], r6.at[i], peers[p - 1]))
        sent.append(send(lows.at[c, x, rows(b)], lows.at[c, x, rows(b)], s5.at[b], r5.at[b], partner))
        product = total * base[rows(b), :]
        pos = position(b)
        for s in range(SEQS):
            inside = (pos >= bounds[s]) & (pos < bounds[s + 1])
            tables[s] = tables[s] + jnp.sum(jnp.where(inside, product, 0.0), axis=0, keepdims=True)

    def forward(b):
        for p in range(1, chips):
            j = lax.rem(x + chips - p, chips)
            i = (p - 1) * nb + b
            arrived(lows.at[c, j, rows(b)], r6.at[i])
            sent.append(send(lows.at[c, j, rows(b)], lows.at[c, j, rows(b)], s7.at[i], r7.at[i], partner))

    project()
    pl.semaphore_wait(barrier, count)
    for b in range(nb):
        to_core(b)
    for copy in small:
        copy.wait()
    segments = seg[...]
    counts = [jnp.sum(jnp.where(segments == s, 1.0, 0.0), axis=1, keepdims=True) for s in range(SEQS)]
    bounds = [jnp.zeros((1, 1), F32)]
    for s in range(SEQS):
        bounds.append(bounds[-1] + counts[s])
    start = jnp.zeros(segments.shape, F32)
    for s in range(1, SEQS):
        start = jnp.where(segments == s, bounds[s], start)
    own_cols = pl.ds(pl.multiple_of(x * HD, HD), HD)
    own_scale = ks[:, own_cols] * (1.0 - cf) + vs[:, own_cols] * cf
    tenant = lax.broadcasted_iota(jnp.int32, (NT, HD), 0)
    scale_rows = [
        jnp.sum(jnp.where(tenant == tenants[0, s], own_scale, 0.0), axis=0, keepdims=True) for s in range(SEQS)]

    for b in range(nb):
        pos = position(b)
        f = jnp.broadcast_to(scale_rows[SEQS - 1], (RB, HD))
        for s in range(SEQS - 2, -1, -1):
            f = jnp.where(pos < bounds[s + 1], scale_rows[s], f)
        factor[rows(b), :] = f
        grads[0, rows(b), :] = jnp.zeros((RB, HD), F32)
        grads[1, rows(b), :] = jnp.zeros((RB, HD), F32)
    for b in range(nb):
        to_chips(b)
    finish(0)
    finish(1)
    pairs = heads // TOGETHER
    for b in range(nb):
        ready(b)
        last = b == nb - 1
        attend(b, 0, pairs // 2 if last else pairs)
        if b + 2 < nb:
            finish(b + 2)
        if last:
            for j in range(nb - 1 - look):
                lows_out(j)
            attend(b, pairs // 2, pairs)
        elif b >= look:
            grads_to_core(b - look)
    for j in range(nb - 1 - look, nb):
        grads_to_core(j)
    for j in range(nb - 1 - look, nb):
        lows_out(j)

    for s in range(SEQS):
        sums[0, c, pl.ds(s, 1), :] = tables[s]
        sums[0, c, pl.ds(SEQS + s, 1), :] = jnp.full((1, HD), 1.0, F32) * tenants[0, s].astype(F32)
    for i in range(ndp):
        if i == 0:
            sent.append(send(sums.at[0, c], sums.at[0, c], sg.at[other], rg.at[c], partner))
        else:
            for core in range(2):
                sent.append(send(
                    sums.at[0, c], sums.at[i, c], sg.at[2 * i + core], rg.at[2 * i + c], (groups[i], 2 * x + core)))
    for b in range(nb):
        forward(b)
    for b in range(nb):
        arrived(lows.at[other, x, rows(b)], r5.at[b])
        for p in range(1, chips):
            j = lax.rem(x + chips - p, chips)
            arrived(lows.at[other, j, rows(b)], r7.at[(p - 1) * nb + b])
    saves = []
    for kind in range(2):
        for h in range(chips):
            n = kind * chips + h
            saves.append(pltpu.make_async_copy(lows.at[kind, h], low_out.at[:, pl.ds(n * HD, HD)], sem_s.at[n]))
            saves[-1].start()
    for i in range(ndp):
        if i == 0:
            arrived(sums.at[0, other], rg.at[other])
        else:
            for core in range(2):
                arrived(sums.at[i, core], rg.at[2 * i + core])
    for i in range(ndp):
        for core in range(2):
            value = sums[i, core]
            turned = jnp.concatenate([value[:, HD // 2:], value[:, :HD // 2]], axis=1)
            sums_out[i, core] = value * (1.0 - cf) + turned * cf
    for copy in saves:
        copy.wait()
    for copy in sent:
        copy.wait_send()


def closing(
    ndp, low_hbm, kw_hbm, vw_hbm, sums, grad_hbm, key_out, value_out, low, kw, vw, grad, sem_l, sem_k, sem_v, sem_g
):
    depth = kw.shape[0]
    block = min(FB, depth)
    count = depth // block

    def load_low():
        return pltpu.make_async_copy(low_hbm, low, sem_l.at[0])

    def at(i):
        return pl.ds(pl.multiple_of(i * block, block), block)

    def load_key(i):
        return pltpu.make_async_copy(kw_hbm.at[at(i)], kw.at[at(i)], sem_k.at[i])

    def load_value(i):
        return pltpu.make_async_copy(vw_hbm.at[at(i)], vw.at[at(i)], sem_v.at[i])

    def save(i):
        return pltpu.make_async_copy(grad.at[:, at(i)], grad_hbm.at[:, at(i)], sem_g.at[i])

    load_low().start()
    for i in range(count):
        load_key(i).start()
        load_value(i).start()
    load_low().wait()

    def step(i, _):
        load_key(i).wait()
        load_value(i).wait()
        wide = kw.shape[1]
        value = dot_nt(low[:, :wide], kw[at(i), :]) + dot_nt(low[:, wide:], vw[at(i), :])
        grad[:, at(i)] = value.astype(BF16)
        save(i).start()
        return 0

    lax.fori_loop(0, count, step, 0)

    tenant = lax.broadcasted_iota(jnp.int32, (NT, HD), 0).astype(F32)
    for kind, out in ((0, key_out), (1, value_out)):
        total = jnp.zeros((NT, HD), F32)
        for i in range(ndp):
            rows = sums[i, kind]
            for s in range(SEQS):
                total = total + jnp.where(tenant == rows[SEQS + s:SEQS + s + 1, :], rows[s:s + 1, :], 0.0)
        out[...] = total[:, :HD // 2]
    for i in range(count):
        save(i).wait()


def on_device(ndp, nten, tokens, queries, out_grad, key_weight, value_weight, key_scale, value_scale, segment_ids, tenant_ids):
    chips = nten // 2
    rows_all, depth = tokens.shape
    nb = rows_all // RB
    wide = key_weight.shape[1]
    hbm = pl.BlockSpec(memory_space=pltpu.HBM)
    vmem = pl.BlockSpec(memory_space=pltpu.VMEM)
    sem = pltpu.SemaphoreType.DMA
    pieces = depth // min(KD, depth)
    many = max(1, (chips - 1) * nb)
    low, sums = pl.pallas_call(
        functools.partial(inner, ndp, nten),
        out_shape=(
            jax.ShapeDtypeStruct((rows_all, 2 * wide), BF16),
            jax.ShapeDtypeStruct((ndp, 2, 2 * SEQS, HD), F32),
        ),
        in_specs=[hbm] * 9,
        out_specs=(hbm, vmem),
        scratch_shapes=[
            pltpu.VMEM(tokens.shape, BF16),
            pltpu.VMEM(queries.shape, BF16),
            pltpu.VMEM(out_grad.shape, BF16),
            pltpu.VMEM(key_weight.shape, BF16),
            pltpu.VMEM(value_weight.shape, BF16),
            pltpu.VMEM((2, chips, rows_all, HD), F32),
            pltpu.VMEM((chips, rows_all, HD), F32),
            pltpu.VMEM((max(1, chips - 1), rows_all, HD), F32),
            pltpu.VMEM((rows_all, HD), F32),
            pltpu.VMEM((2, rows_all, HD), BF16),
            pltpu.VMEM((rows_all, HD), F32),
            pltpu.VMEM((LONGEST + RB, RB), F32),
            pltpu.VMEM((2, rows_all, HD), F32),
            pltpu.VMEM((rows_all, HD), F32),
            pltpu.VMEM((2, chips, rows_all, HD), BF16),
            pltpu.VMEM((ndp, 2, 2 * SEQS, HD), F32),
            pltpu.VMEM(key_scale.shape, F32),
            pltpu.VMEM(value_scale.shape, F32),
            pltpu.VMEM(segment_ids.shape, jnp.int32),
            pltpu.SMEM(tenant_ids.shape, jnp.int32),
            sem((2 * pieces,)), sem((pieces,)), sem((nb,)), sem((nb,)), sem((4,)), sem((2 * chips,)),
            sem((nb,)), sem((nb,)), sem((many,)), sem((many,)), sem((nb,)), sem((nb,)), sem((nb,)), sem((nb,)),
            sem((nb,)), sem((nb,)), sem((many,)), sem((many,)), sem((many,)), sem((many,)),
            sem((2 * ndp,)), sem((2 * ndp,)),
        ],
        compiler_params=pltpu.CompilerParams(
            collective_id=0, has_side_effects=True, vmem_limit_bytes=VMEM_LIMIT),
    )(tokens, queries, out_grad, key_weight, value_weight, key_scale, value_scale, segment_ids, tenant_ids)

    count = depth // min(FB, depth)
    return pl.pallas_call(
        functools.partial(closing, ndp),
        out_shape=(
            jax.ShapeDtypeStruct((rows_all, depth), BF16),
            jax.ShapeDtypeStruct((NT, HD // 2), F32),
            jax.ShapeDtypeStruct((NT, HD // 2), F32),
        ),
        in_specs=[hbm] * 3 + [vmem],
        out_specs=(hbm, vmem, vmem),
        scratch_shapes=[
            pltpu.VMEM((rows_all, 2 * wide), BF16),
            pltpu.VMEM(key_weight.shape, BF16),
            pltpu.VMEM(value_weight.shape, BF16),
            pltpu.VMEM((rows_all, depth), BF16),
            sem((1,)), sem((count,)), sem((count,)), sem((count,)),
        ],
        compiler_params=pltpu.CompilerParams(vmem_limit_bytes=VMEM_LIMIT),
    )(low, key_weight, value_weight, sums)


def solution(mesh):
    return jax.shard_map(
        functools.partial(on_device, mesh.shape["dp"], mesh.shape["tensor"]),
        mesh=mesh,
        in_specs=(
            P("dp", "tensor"),
            P("dp", "tensor"),
            P("dp", "tensor"),
            P("tensor", None),
            P("tensor", None),
            P(),
            P(),
            P("dp", None),
            P("dp", None),
        ),
        out_specs=(P("dp", "tensor"), P(None, "tensor"), P(None, "tensor")),
        check_vma=False,
    )
```

```python
import functools
import math

import jax
import jax.numpy as jnp
from jax import lax
from jax.experimental import pallas as pl
from jax.experimental.pallas import tpu as pltpu
from jax.sharding import PartitionSpec as P

MESH = pl.DeviceIdType.MESH
F32 = jnp.float32
BF16 = jnp.bfloat16
SEQS = 4
NT = 32
HD = 128
RB = 128
LONGEST = 256
VMEM_LIMIT = 64 * 1024 * 1024
TOGETHER = 4
FB = 1024
KC = 4


def dot_nt(a, b):
    return lax.dot_general(a, b, (((1,), (1,)), ((), ())), preferred_element_type=F32)


def dot_nn(a, b):
    return jnp.dot(a, b, preferred_element_type=F32)


def inner(
    ndp, nten, tok_hbm, q_hbm, o_hbm, kw_hbm, vw_hbm, ks_hbm, vs_hbm, seg_hbm, tenants_hbm,
    low_out, sums_out,
    tok, q, o, kw, vw, part, from_core, from_chip, base, kv, factor, bias, grads, grads_in, lows, sums,
    ks, vs, seg, tenants,
    sem_w, sem_t, sem_q, sem_o, sem_p, sem_s,
    s1, r1, s2, r2, s3, r3, s4, r4, s5, r5, s6, r6, s7, r7, sg, rg,
):
    chips = nten // 2
    rows_all, depth = tok.shape
    nb = rows_all // RB
    look = LONGEST // RB
    half = rows_all // 2
    kc = depth // KC
    d = lax.axis_index("dp")
    t = lax.axis_index("tensor")
    x = t // 2
    c = lax.rem(t, 2)
    other = 1 - c
    cf = c.astype(F32)
    partner = (d, 2 * x + other)
    peers = [(d, 2 * lax.rem(x + p, chips) + c) for p in range(1, chips)]
    groups = [lax.rem(d + i, ndp) for i in range(ndp)]

    def rows(b):
        return pl.ds(b * RB, RB)

    def load(src, dst, at, cols, sem):
        return pltpu.make_async_copy(src.at[at, cols], dst.at[at, cols], sem)

    loads = {}
    for b in range(nb):
        loads["q", b] = pltpu.make_async_copy(q_hbm.at[rows(b)], q.at[rows(b)], sem_q.at[b])
        loads["o", b] = pltpu.make_async_copy(o_hbm.at[rows(b)], o.at[rows(b)], sem_o.at[b])
    small = [
        pltpu.make_async_copy(src, dst, sem_p.at[i])
        for i, (src, dst) in enumerate(((ks_hbm, ks), (vs_hbm, vs), (seg_hbm, seg), (tenants_hbm, tenants)))]
    for copy in small:
        copy.start()
    load(tok_hbm, tok, pl.ds(0, half), slice(None), sem_t.at[0]).start()
    for k in range(KC):
        kk = pl.ds(k * kc, kc)
        load(kw_hbm, kw, kk, slice(None), sem_w.at[k]).start()
        load(vw_hbm, vw, kk, slice(None), sem_w.at[KC + k]).start()
    load(tok_hbm, tok, pl.ds(half, half), slice(None), sem_t.at[1]).start()
    for b in range(nb):
        loads["q", b].start()
        loads["o", b].start()

    barrier = pltpu.get_barrier_semaphore()
    count = 0
    for dev in [partner] + peers:
        pl.semaphore_signal(barrier, inc=1, device_id=dev, device_id_type=MESH)
        count += 1
    for i in range(1, ndp):
        for core in range(2):
            pl.semaphore_signal(barrier, inc=1, device_id=(groups[i], 2 * x + core), device_id_type=MESH)
            count += 1

    def send(src, dst, ssem, rsem, dev):
        copy = pltpu.make_async_remote_copy(
            src_ref=src, dst_ref=dst, send_sem=ssem, recv_sem=rsem, device_id=dev, device_id_type=MESH)
        copy.start()
        return copy

    def arrived(dst, rsem):
        pltpu.make_async_remote_copy(
            src_ref=dst, dst_ref=dst, send_sem=s1.at[0], recv_sem=rsem, device_id=partner, device_id_type=MESH
        ).wait_recv()

    sent = []

    def project(r, lo, hi):
        rr = pl.ds(r * half, half)

        if lo == 0:
            load(tok_hbm, tok, rr, slice(None), sem_t.at[r]).wait()

        def step(k, first):
            kk = pl.ds(pl.multiple_of(k * kc, kc), kc)
            if r == 0:
                load(kw_hbm, kw, kk, slice(None), sem_w.at[k]).wait()
                load(vw_hbm, vw, kk, slice(None), sem_w.at[KC + k]).wait()
            block = tok[rr, kk]
            for kind, weight in ((0, kw), (1, vw)):
                value = dot_nn(block, weight[kk, :])
                for h in range(chips):
                    piece = value[:, h * HD:(h + 1) * HD]
                    part[kind, h, rr, :] = piece if first else piece + part[kind, h, rr, :]

        if lo == 0:
            step(0, True)

        def more(k, _):
            step(k, False)
            return 0

        lax.fori_loop(max(lo, 1), hi, more, 0)

    def to_core(b):
        sent.append(send(part.at[other, :, rows(b)], from_core.at[:, rows(b)], s1.at[b], r1.at[b], partner))

    def to_chips(b):
        arrived(from_core.at[:, rows(b)], r1.at[b])
        for p in range(1, chips):
            j = lax.rem(x + p, chips)
            part[c, j, rows(b), :] = part[c, j, rows(b), :] + from_core[j, rows(b), :]
            i = (p - 1) * nb + b
            sent.append(send(part.at[c, j, rows(b)], from_chip.at[p - 1, rows(b)], s2.at[i], r2.at[i], peers[p - 1]))

    def position(b):
        return lax.broadcasted_iota(jnp.int32, (RB, HD), 0).astype(F32) + float(b * RB)

    def finish(b):
        total = part[c, x, rows(b), :] + from_core[x, rows(b), :]
        for p in range(1, chips):
            arrived(from_chip.at[p - 1, rows(b)], r2.at[(p - 1) * nb + b])
            total = total + from_chip[p - 1, rows(b), :]
        base[rows(b), :] = total
        kv[c, rows(b), :] = (total * factor[rows(b), :]).astype(BF16)
        sent.append(send(kv.at[c, rows(b)], kv.at[c, rows(b)], s3.at[b], r3.at[b], partner))

    heads = q.shape[1] // HD
    score_scale = HD ** -0.5
    to_exp2 = score_scale * math.log2(math.e)

    def ready(b):
        arrived(kv.at[other, rows(b)], r3.at[b])
        loads["q", b].wait()
        loads["o", b].wait()
        first = max(0, b - look)
        query_pos = lax.broadcasted_iota(jnp.int32, (RB, RB), 1).astype(F32) + float(b * RB)
        begin = start[:, b * RB:(b + 1) * RB]
        for j in range(first, b + 1):
            key_pos = position(j)
            seen = (key_pos >= begin) & (key_pos <= query_pos)
            bias[rows(j - first), :] = jnp.where(seen, 0.0, -1e30)

    def attend(b, lo, hi):
        first = max(0, b - look)
        width = (b + 1 - first) * RB
        keys_at = pl.ds(first * RB, width)

        def several(i, _):
            cols = [pl.ds(pl.multiple_of((i * TOGETHER + n) * HD, HD), HD) for n in range(TOGETHER)]
            keys, values, hidden = kv[0, keys_at, :], kv[1, keys_at, :], bias[pl.ds(0, width), :]
            qs, outs, lows_, score_grads = [], [], [], []
            for col in cols:
                qh, oh = q[rows(b), col], o[rows(b), col]
                scores = dot_nt(keys, qh) + hidden
                grad = dot_nt(values, oh)
                peak = jnp.max(scores, axis=0, keepdims=True)
                e = jnp.exp2((scores - peak) * to_exp2)
                probs = e * (1.0 / jnp.sum(e, axis=0, keepdims=True))
                low = probs.astype(BF16)
                delta = jnp.sum(low.astype(F32) * grad, axis=0, keepdims=True)
                qs.append(qh)
                outs.append(oh)
                lows_.append(low)
                score_grads.append((probs * (grad - delta)).astype(BF16))
            grads[1, keys_at, :] = grads[1, keys_at, :] + dot_nn(
                jnp.concatenate(lows_, axis=1), jnp.concatenate(outs, axis=0))
            grads[0, keys_at, :] = grads[0, keys_at, :] + dot_nn(
                jnp.concatenate(score_grads, axis=1), jnp.concatenate(qs, axis=0))
            return 0

        lax.fori_loop(lo, hi, several, 0)

    def grads_to_core(b):
        sent.append(send(grads.at[other, rows(b)], grads_in.at[rows(b)], s4.at[b], r4.at[b], partner))

    tables = [jnp.zeros((1, HD), F32) for s in range(SEQS)]

    def lows_out(b):
        arrived(grads_in.at[rows(b)], r4.at[b])
        total = (grads[c, rows(b), :] + grads_in[rows(b), :]) * (cf + (1.0 - cf) * score_scale)
        lows[c, x, rows(b), :] = (total * factor[rows(b), :]).astype(BF16)
        for p in range(1, chips):
            i = (p - 1) * nb + b
            sent.append(send(lows.at[c, x, rows(b)], lows.at[c, x, rows(b)], s6.at[i], r6.at[i], peers[p - 1]))
        sent.append(send(lows.at[c, x, rows(b)], lows.at[c, x, rows(b)], s5.at[b], r5.at[b], partner))
        product = total * base[rows(b), :]
        pos = position(b)
        for s in range(SEQS):
            inside = (pos >= bounds[s]) & (pos < bounds[s + 1])
            tables[s] = tables[s] + jnp.sum(jnp.where(inside, product, 0.0), axis=0, keepdims=True)

    def forward(b):
        for p in range(1, chips):
            j = lax.rem(x + chips - p, chips)
            i = (p - 1) * nb + b
            arrived(lows.at[c, j, rows(b)], r6.at[i])
            sent.append(send(lows.at[c, j, rows(b)], lows.at[c, j, rows(b)], s7.at[i], r7.at[i], partner))

    project(0, 0, KC)
    pl.semaphore_wait(barrier, count)
    for b in range(nb // 2):
        to_core(b)
    for copy in small:
        copy.wait()
    segments = seg[...]
    counts = [jnp.sum(jnp.where(segments == s, 1.0, 0.0), axis=1, keepdims=True) for s in range(SEQS)]
    bounds = [jnp.zeros((1, 1), F32)]
    for s in range(SEQS):
        bounds.append(bounds[-1] + counts[s])
    start = jnp.zeros(segments.shape, F32)
    for s in range(1, SEQS):
        start = jnp.where(segments == s, bounds[s], start)
    own_cols = pl.ds(pl.multiple_of(x * HD, HD), HD)
    own_scale = ks[:, own_cols] * (1.0 - cf) + vs[:, own_cols] * cf
    tenant = lax.broadcasted_iota(jnp.int32, (NT, HD), 0)
    scale_rows = [
        jnp.sum(jnp.where(tenant == tenants[0, s], own_scale, 0.0), axis=0, keepdims=True) for s in range(SEQS)]

    for b in range(nb):
        pos = position(b)
        f = jnp.broadcast_to(scale_rows[SEQS - 1], (RB, HD))
        for s in range(SEQS - 2, -1, -1):
            f = jnp.where(pos < bounds[s + 1], scale_rows[s], f)
        factor[rows(b), :] = f
        grads[0, rows(b), :] = jnp.zeros((RB, HD), F32)
        grads[1, rows(b), :] = jnp.zeros((RB, HD), F32)
    project(1, 0, KC // 2)
    for b in range(nb // 2):
        to_chips(b)
    project(1, KC // 2, KC)
    for b in range(nb // 2, nb):
        to_core(b)
    for b in range(nb // 2, nb):
        to_chips(b)
    finish(0)
    finish(1)
    pairs = heads // TOGETHER
    for b in range(nb):
        ready(b)
        last = b == nb - 1
        attend(b, 0, pairs // 2 if last else pairs)
        if b + 2 < nb:
            finish(b + 2)
        if last:
            for j in range(nb - 1 - look):
                lows_out(j)
            attend(b, pairs // 2, pairs)
        elif b >= look:
            grads_to_core(b - look)
    for j in range(nb - 1 - look, nb):
        grads_to_core(j)
    for j in range(nb - 1 - look, nb):
        lows_out(j)

    for s in range(SEQS):
        sums[0, c, pl.ds(s, 1), :] = tables[s]
        sums[0, c, pl.ds(SEQS + s, 1), :] = jnp.full((1, HD), 1.0, F32) * tenants[0, s].astype(F32)
    for i in range(ndp):
        if i == 0:
            sent.append(send(sums.at[0, c], sums.at[0, c], sg.at[other], rg.at[c], partner))
        else:
            for core in range(2):
                sent.append(send(
                    sums.at[0, c], sums.at[i, c], sg.at[2 * i + core], rg.at[2 * i + c], (groups[i], 2 * x + core)))
    for b in range(nb):
        forward(b)
    for b in range(nb):
        arrived(lows.at[other, x, rows(b)], r5.at[b])
        for p in range(1, chips):
            j = lax.rem(x + chips - p, chips)
            arrived(lows.at[other, j, rows(b)], r7.at[(p - 1) * nb + b])
    saves = []
    for kind in range(2):
        for h in range(chips):
            n = kind * chips + h
            saves.append(pltpu.make_async_copy(lows.at[kind, h], low_out.at[:, pl.ds(n * HD, HD)], sem_s.at[n]))
            saves[-1].start()
    for i in range(ndp):
        if i == 0:
            arrived(sums.at[0, other], rg.at[other])
        else:
            for core in range(2):
                arrived(sums.at[i, core], rg.at[2 * i + core])
    for i in range(ndp):
        for core in range(2):
            value = sums[i, core]
            turned = jnp.concatenate([value[:, HD // 2:], value[:, :HD // 2]], axis=1)
            sums_out[i, core] = value * (1.0 - cf) + turned * cf
    for copy in saves:
        copy.wait()
    for copy in sent:
        copy.wait_send()


def closing(
    ndp, low_hbm, kw_hbm, vw_hbm, sums, grad_hbm, key_out, value_out, low, kw, vw, grad, sem_l, sem_k, sem_v, sem_g
):
    depth = kw.shape[0]
    block = min(FB, depth)
    count = depth // block

    def load_low():
        return pltpu.make_async_copy(low_hbm, low, sem_l.at[0])

    def at(i):
        return pl.ds(pl.multiple_of(i * block, block), block)

    def load_key(i):
        return pltpu.make_async_copy(kw_hbm.at[at(i)], kw.at[at(i)], sem_k.at[i])

    def load_value(i):
        return pltpu.make_async_copy(vw_hbm.at[at(i)], vw.at[at(i)], sem_v.at[i])

    half = grad.shape[0] // 2
    group = min(2 * block, depth)

    def save(r, g):
        at_ = (pl.ds(r * half, half), pl.ds(g * group, group))
        return pltpu.make_async_copy(grad.at[at_], grad_hbm.at[at_], sem_g.at[r * (depth // group) + g])

    load_low().start()
    for i in range(count):
        load_key(i).start()
        load_value(i).start()
    load_low().wait()

    wide = kw.shape[1]
    saves = []
    for r in range(2):
        rr = pl.ds(r * half, half)

        def step(i, _):
            if r == 0:
                load_key(i).wait()
                load_value(i).wait()
            value = dot_nt(low[rr, :wide], kw[at(i), :]) + dot_nt(low[rr, wide:], vw[at(i), :])
            grad[rr, at(i)] = value.astype(BF16)
            return 0

        for g in range(depth // group):
            each = group // block
            lax.fori_loop(g * each, (g + 1) * each, step, 0)
            saves.append(save(r, g))
            saves[-1].start()

    tenant = lax.broadcasted_iota(jnp.int32, (NT, HD), 0).astype(F32)
    for kind, out in ((0, key_out), (1, value_out)):
        total = jnp.zeros((NT, HD), F32)
        for i in range(ndp):
            rows = sums[i, kind]
            for s in range(SEQS):
                total = total + jnp.where(tenant == rows[SEQS + s:SEQS + s + 1, :], rows[s:s + 1, :], 0.0)
        out[...] = total[:, :HD // 2]
    for copy in saves:
        copy.wait()


def on_device(ndp, nten, tokens, queries, out_grad, key_weight, value_weight, key_scale, value_scale, segment_ids, tenant_ids):
    chips = nten // 2
    rows_all, depth = tokens.shape
    nb = rows_all // RB
    wide = key_weight.shape[1]
    hbm = pl.BlockSpec(memory_space=pltpu.HBM)
    vmem = pl.BlockSpec(memory_space=pltpu.VMEM)
    sem = pltpu.SemaphoreType.DMA
    many = max(1, (chips - 1) * nb)
    low, sums = pl.pallas_call(
        functools.partial(inner, ndp, nten),
        out_shape=(
            jax.ShapeDtypeStruct((rows_all, 2 * wide), BF16),
            jax.ShapeDtypeStruct((ndp, 2, 2 * SEQS, HD), F32),
        ),
        in_specs=[hbm] * 9,
        out_specs=(hbm, vmem),
        scratch_shapes=[
            pltpu.VMEM(tokens.shape, BF16),
            pltpu.VMEM(queries.shape, BF16),
            pltpu.VMEM(out_grad.shape, BF16),
            pltpu.VMEM(key_weight.shape, BF16),
            pltpu.VMEM(value_weight.shape, BF16),
            pltpu.VMEM((2, chips, rows_all, HD), F32),
            pltpu.VMEM((chips, rows_all, HD), F32),
            pltpu.VMEM((max(1, chips - 1), rows_all, HD), F32),
            pltpu.VMEM((rows_all, HD), F32),
            pltpu.VMEM((2, rows_all, HD), BF16),
            pltpu.VMEM((rows_all, HD), F32),
            pltpu.VMEM((LONGEST + RB, RB), F32),
            pltpu.VMEM((2, rows_all, HD), F32),
            pltpu.VMEM((rows_all, HD), F32),
            pltpu.VMEM((2, chips, rows_all, HD), BF16),
            pltpu.VMEM((ndp, 2, 2 * SEQS, HD), F32),
            pltpu.VMEM(key_scale.shape, F32),
            pltpu.VMEM(value_scale.shape, F32),
            pltpu.VMEM(segment_ids.shape, jnp.int32),
            pltpu.SMEM(tenant_ids.shape, jnp.int32),
            sem((2 * KC,)), sem((2,)), sem((nb,)), sem((nb,)), sem((4,)), sem((2 * chips,)),
            sem((nb,)), sem((nb,)), sem((many,)), sem((many,)), sem((nb,)), sem((nb,)), sem((nb,)), sem((nb,)),
            sem((nb,)), sem((nb,)), sem((many,)), sem((many,)), sem((many,)), sem((many,)),
            sem((2 * ndp,)), sem((2 * ndp,)),
        ],
        compiler_params=pltpu.CompilerParams(
            collective_id=0, has_side_effects=True, vmem_limit_bytes=VMEM_LIMIT),
    )(tokens, queries, out_grad, key_weight, value_weight, key_scale, value_scale, segment_ids, tenant_ids)

    count = depth // min(FB, depth)
    return pl.pallas_call(
        functools.partial(closing, ndp),
        out_shape=(
            jax.ShapeDtypeStruct((rows_all, depth), BF16),
            jax.ShapeDtypeStruct((NT, HD // 2), F32),
            jax.ShapeDtypeStruct((NT, HD // 2), F32),
        ),
        in_specs=[hbm] * 3 + [vmem],
        out_specs=(hbm, vmem, vmem),
        scratch_shapes=[
            pltpu.VMEM((rows_all, 2 * wide), BF16),
            pltpu.VMEM(key_weight.shape, BF16),
            pltpu.VMEM(value_weight.shape, BF16),
            pltpu.VMEM((rows_all, depth), BF16),
            sem((1,)), sem((count,)), sem((count,)), sem((2 * count,)),
        ],
        compiler_params=pltpu.CompilerParams(vmem_limit_bytes=VMEM_LIMIT),
    )(low, key_weight, value_weight, sums)


def solution(mesh):
    return jax.shard_map(
        functools.partial(on_device, mesh.shape["dp"], mesh.shape["tensor"]),
        mesh=mesh,
        in_specs=(
            P("dp", "tensor"),
            P("dp", "tensor"),
            P("dp", "tensor"),
            P("tensor", None),
            P("tensor", None),
            P(),
            P(),
            P("dp", None),
            P("dp", None),
        ),
        out_specs=(P("dp", "tensor"), P(None, "tensor"), P(None, "tensor")),
        check_vma=False,
    )
```
